32 devices in a mesh: dp: 8 (over y, x, core), mp: 4 (over z).
Axes of the slice: x: 2, y: 2, z: 4, core: 2. Of those that a mesh axis runs over, the one named last changes fastest.
Arguments:
- weight: bfloat16 [128, 128, 128], P(('dp', 'mp')), may hold values from -6 to 6
- moment_one: float32 [128, 128, 128], P(('dp', 'mp')), may hold values from -1.8 to 1.8
- moment_two: float32 [128, 128, 128], P(('dp', 'mp')), may hold values from 0.01 to 1
- block_row: int32 [128], P(('dp', 'mp')), may hold values from 0 to 63, as said below
- block_col: int32 [128], P(('dp', 'mp')), may hold values from 0 to 55
- dest_slot: int32 [128], P(('dp', 'mp')), may hold values from -1 to 31, as said below
- tokens: bfloat16 [1024, 8192], P('dp', 'mp'), may hold values from -6 to 6
- upstream: bfloat16 [1024, 28672], P('dp', 'mp'), may hold values from -6 to 6
Outputs:
- new_weight: bfloat16 [128, 128, 128], P(('dp', 'mp'))
- new_first: float32 [128, 128, 128], P(('dp', 'mp'))
- new_second: float32 [128, 128, 128], P(('dp', 'mp'))
- hidden_out: bfloat16 [1024, 28672], P('dp', 'mp')
- input_grad: bfloat16 [1024, 8192], P('dp', 'mp')
The draws below stay inside these ranges and needn't reach their ends.
Inputs may be any that keep to these rules, and one draw needn't show every extreme that they name: Within one tensor slice the pairs (block_row, block_col) are distinct. `dest_slot`: within one tensor slice the non-negative values are distinct; slots d * 4 to (d + 1) * 4 - 1 belong to dp index d, and a block held by dp index d goes to d - 1, d or d + 1; at most 2 blocks of one device go to each neighbour, and in every slice some pair of neighbours exchanges exactly 2 blocks each way.
All inputs are finite; a program needn't handle non-finite values.
Results may differ from the reference program's by a relative error of at most 0.0055.
Values may be sent and summed in bfloat16 or wider, within the bound.
No kernel may reach another device: no remote copies, remote signals or barrier semaphores. Data moves between devices by JAX's collectives and lax.ppermute only.
A program may use at most 128 MiB of HBM per device.

```python
import math
import jax
import jax.numpy as jnp
from jax import lax

D = 8192
FF = 28672
BS = 128
KEPT_DEV = 4
TOKENS = 1024
KEPT = 32
SLICES = 4
KEPT_ALL = 128
BLOCK_ROWS = 64
BLOCK_COLS = 56


def block_positions(key):
    slice_count = KEPT_ALL // KEPT
    column_count = FF // (BS * slice_count)
    positions_all = D // BS * column_count

    def one_slice(slice_index):
        slice_key = jax.random.fold_in(key, slice_index)
        first_key, second_key = jax.random.split(slice_key)
        inner_part = jax.random.permutation(first_key, positions_all - 2).astype(jnp.int32) + 1
        chosen = jnp.concatenate([jnp.array([0, positions_all - 1], dtype=jnp.int32), inner_part[:KEPT - 2]])
        return chosen[jax.random.permutation(second_key, KEPT)]
    position_list = jax.vmap(one_slice)(jnp.arange(slice_count, dtype=jnp.int32))
    position_list = jnp.swapaxes(position_list.reshape(slice_count, KEPT // KEPT_DEV, KEPT_DEV), 0, 1).reshape(KEPT_ALL)
    return (position_list, column_count)


def draw_block_row(key, part):
    position_list, column_count = block_positions(jax.random.fold_in(key, 101))
    return (position_list // column_count).astype(jnp.int32)


def draw_block_col(key, part):
    position_list, column_count = block_positions(jax.random.fold_in(key, 101))
    return (position_list % column_count).astype(jnp.int32)


def device_permutations(key, device_count):

    def permute_one(key_piece):
        return jax.random.permutation(key_piece, KEPT_DEV).astype(jnp.int32)
    return jax.vmap(permute_one)(jax.random.split(key, device_count))


def draw_dest_slot(key, part):
    slice_count = KEPT_ALL // KEPT
    device_count = KEPT // KEPT_DEV
    half_slots = KEPT_DEV // 2

    def one_slice(slice_index):
        base_key = jax.random.fold_in(jax.random.fold_in(key, 202), slice_index)
        key_list = jax.random.split(base_key, 5)
        crossing = jax.random.randint(key_list[0], (device_count,), 0, half_slots + 1).astype(jnp.int32)
        forced = jax.random.randint(key_list[1], (), 0, device_count - 1)
        device_ids = jnp.arange(device_count, dtype=jnp.int32)
        crossing = jnp.where(device_ids == forced, half_slots, crossing)
        crossing = jnp.where(device_ids == device_count - 1, 0, crossing)
        right_count = crossing[:, None]
        left_count = jnp.concatenate([jnp.zeros((1,), jnp.int32), crossing[:-1]])[:, None]
        ranking = device_permutations(key_list[2], device_count)
        going_left = ranking < left_count
        going_right = (ranking >= left_count) & (ranking < left_count + right_count)
        target = device_ids[:, None] + going_right.astype(jnp.int32) - going_left.astype(jnp.int32)
        item = jnp.where(going_left, KEPT_DEV - left_count + ranking, jnp.where(going_right, ranking - left_count, ranking - right_count))
        slot_order = device_permutations(key_list[3], device_count)
        new_slot = target * KEPT_DEV + slot_order[target, item]
        staying = jnp.logical_not(going_left | going_right)
        dropped = staying & (jax.random.randint(key_list[4], (device_count, KEPT_DEV), 0, 6) == 0) & (new_slot != KEPT - 1)
        forced_drop = staying & (device_ids[:, None] == 0) & (ranking == right_count)
        return jnp.where(dropped | forced_drop, -1, new_slot).astype(jnp.int32)
    slot_list = jax.vmap(one_slice)(jnp.arange(slice_count, dtype=jnp.int32))
    return jnp.swapaxes(slot_list, 0, 1).reshape(KEPT_ALL)


def shard_levels(stream_key, dims, cuts, least, high):
    level = 1.0
    for axis_at, parts in cuts:
        steps = jax.random.uniform(jax.random.fold_in(jax.random.fold_in(stream_key, 6), axis_at), (parts,), jnp.float32, least / len(cuts), high / len(cuts))
        level = level * jnp.repeat(jnp.exp(steps), dims[axis_at] // parts).reshape((-1,) + (1,) * (len(dims) - 1 - axis_at))
    return level


def normal_values(own_key, extent, scale, reach, shards=(), kind=jnp.bfloat16):
    values = jax.random.normal(own_key, extent, jnp.float32) * scale
    if len(shards) > 0:
        values = shard_levels(own_key, extent, shards, -0.22, 0.18) * values
    return jnp.clip(values, min=-reach, max=reach).astype(kind)


def setup_inputs(seed: int = 0) -> dict:
    seeds = jax.random.split(jax.random.key(seed), 9)
    return {
        "weight": normal_values(seeds[0], (KEPT_ALL, BS, BS), 1.0, 6.0, ((0, 32),)),
        "moment_one": normal_values(seeds[1], (KEPT_ALL, BS, BS), 0.3, 1.8, ((0, 32),), jnp.float32),
        "moment_two": jnp.clip(jnp.exp(math.log(1.0) - 4.6051702 * jax.random.uniform(seeds[2], (KEPT_ALL, BS, BS), jnp.float32) ** shard_levels(seeds[2], (KEPT_ALL, BS, BS), ((0, 32),), -0.2, 0.2)), 0.01, 1.0),
        "block_row": draw_block_row(jax.random.fold_in(seeds[8], 71), 0),
        "block_col": draw_block_col(jax.random.fold_in(seeds[8], 71), 0),
        "dest_slot": draw_dest_slot(jax.random.fold_in(seeds[8], 71), 0),
        "tokens": normal_values(seeds[6], (TOKENS, D), 1.0, 6.0, ((0, 8), (1, 4))),
        "upstream": normal_values(seeds[7], (TOKENS, FF), 1.0, 6.0, ((0, 8), (1, 4))),
    }


learn_rate = 0.02
beta_first = 0.9
beta_second = 0.95
epsilon = 1e-08
highest = lax.Precision.HIGHEST

def slice_view(array):
    rest_shape = array.shape[1:]
    grouped = array.reshape((KEPT // KEPT_DEV, SLICES, KEPT_DEV) + rest_shape)
    return jnp.swapaxes(grouped, 0, 1).reshape((SLICES, KEPT) + rest_shape)

def slice_unview(array):
    rest_shape = array.shape[2:]
    grouped = array.reshape((SLICES, KEPT // KEPT_DEV, KEPT_DEV) + rest_shape)
    return jnp.swapaxes(grouped, 0, 1).reshape((KEPT_ALL,) + rest_shape)

def reference(weight, moment_one, moment_two, block_row, block_col, dest_slot, tokens, upstream):
    grad_scale = 1.0 / math.sqrt(D)
    token_view = tokens.reshape(TOKENS, BLOCK_ROWS, BS)
    upstream_view = jnp.swapaxes(upstream.reshape(TOKENS, SLICES, BLOCK_COLS * BS), 0, 1)

    def one_slice(carry, pieces):
        slice_weight, slice_first, slice_second, slice_rows, slice_cols, slice_dest, slice_upstream = pieces
        x_blocks = jnp.take(token_view, slice_rows, axis=1).astype(jnp.float32)
        d_blocks = jnp.take(slice_upstream.reshape(TOKENS, BLOCK_COLS, BS), slice_cols, axis=1).astype(jnp.float32)
        w_float = slice_weight.astype(jnp.float32)
        forward = jnp.einsum('tbk,bkj->tbj', x_blocks, w_float, precision=highest)
        col_sums = jax.ops.segment_sum(jnp.swapaxes(forward, 0, 1), slice_cols, num_segments=BLOCK_COLS)
        hidden = (jnp.swapaxes(col_sums, 0, 1) * grad_scale).reshape(TOKENS, BLOCK_COLS * BS).astype(jnp.bfloat16)
        backward = jnp.einsum('tbj,bkj->tbk', d_blocks, w_float, precision=highest)
        row_sums = jax.ops.segment_sum(jnp.swapaxes(backward, 0, 1), slice_rows, num_segments=BLOCK_ROWS)
        partial_in = jnp.swapaxes(row_sums, 0, 1).reshape(TOKENS, D) * grad_scale
        gradient = jnp.einsum('tbk,tbj->bkj', x_blocks, d_blocks, precision=highest) * grad_scale
        first_new = beta_first * slice_first + (1.0 - beta_first) * gradient
        second_new = beta_second * slice_second + (1.0 - beta_second) * gradient * gradient
        stepped = (w_float - learn_rate * first_new / (jnp.sqrt(second_new) + epsilon)).astype(jnp.bfloat16)
        target_slot = jnp.where(slice_dest >= 0, slice_dest, KEPT).astype(jnp.int32)
        placed_weight = jnp.zeros((KEPT, BS, BS), jnp.bfloat16).at[target_slot].set(stepped, mode='drop')
        placed_first = jnp.zeros((KEPT, BS, BS), jnp.float32).at[target_slot].set(first_new, mode='drop')
        placed_second = jnp.zeros((KEPT, BS, BS), jnp.float32).at[target_slot].set(second_new, mode='drop')
        return (carry + partial_in, (hidden, placed_weight, placed_first, placed_second))
    pieces_all = (slice_view(weight), slice_view(moment_one), slice_view(moment_two), slice_view(block_row), slice_view(block_col), slice_view(dest_slot), upstream_view)
    input_sum, outputs = lax.scan(one_slice, jnp.zeros((TOKENS, D), jnp.float32), pieces_all)
    hidden_all, weight_all, first_all, second_all = outputs
    hidden_out = jnp.swapaxes(hidden_all, 0, 1).reshape(TOKENS, FF)
    return (slice_unview(weight_all), slice_unview(first_all), slice_unview(second_all), hidden_out, input_sum.astype(jnp.bfloat16))
```

```python
import functools
import math

import jax
import jax.numpy as jnp
from jax import lax
from jax.experimental import pallas as pl
from jax.experimental.pallas import tpu as pltpu
from jax.sharding import PartitionSpec as P

D = 8192
TILE = 16
VMEM_LIMIT = 48 * 1024 * 1024

learn_rate = 0.02
beta_first = 0.9
beta_second = 0.95
epsilon = 1e-08
grad_scale = 1.0 / math.sqrt(D)

f32 = jnp.float32
bf16 = jnp.bfloat16
VMEM = pl.BlockSpec(memory_space=pltpu.VMEM)
SMEM = pl.BlockSpec(memory_space=pltpu.SMEM)


def params():
    return pltpu.CompilerParams(vmem_limit_bytes=VMEM_LIMIT)


def lanes(ref, index, width):
    return ref[:, pl.ds(pl.multiple_of(index * width, width), width)]


def pack_kernel(row_s, col_s, dest_s, w_ref, one_ref, two_ref, pack_ref, left_ref, right_ref):
    kept, side = w_ref.shape[0], w_ref.shape[1]
    half = kept // 2
    me = lax.axis_index("dp")
    lane = lax.broadcasted_iota(jnp.int32, (TILE, side), 1)
    pitch = side + TILE
    travel = 3 * side
    left_ref[...] = jnp.zeros_like(left_ref)
    right_ref[...] = jnp.zeros_like(right_ref)
    to_left = jnp.int32(0)
    to_right = jnp.int32(0)
    for s in range(kept):
        dest = dest_s[s]
        tile = jnp.where(lane == 0, row_s[s], jnp.where(lane == 1, col_s[s], dest))
        pack_ref[s * pitch : s * pitch + side, :] = w_ref[s]
        pack_ref[s * pitch + side : (s + 1) * pitch, :] = tile.astype(f32).astype(bf16)
        goal = jnp.where(dest >= 0, dest // kept, me)
        for ref, count, going in (
            (left_ref, to_left, goal < me),
            (right_ref, to_right, goal > me),
        ):

            @pl.when(going)
            def _(ref=ref, count=count, s=s):
                base = pl.multiple_of(jnp.minimum(count, half - 1) * travel, TILE)
                ref[pl.ds(base, side), :] = w_ref[s]
                ref[pl.ds(base + side, side), :] = one_ref[s].astype(bf16)
                ref[pl.ds(base + 2 * side, side), :] = two_ref[s].astype(bf16)

        to_left = to_left + (goal < me).astype(jnp.int32)
        to_right = to_right + (goal > me).astype(jnp.int32)


def pack(rows, cols, dests, weight, one, two):
    kept, side, _ = weight.shape
    travel = jax.ShapeDtypeStruct((kept // 2 * 3 * side, side), bf16)
    return pl.pallas_call(
        pack_kernel,
        out_shape=(jax.ShapeDtypeStruct((kept * (side + TILE), side), bf16), travel, travel),
        in_specs=[SMEM, SMEM, SMEM, VMEM, VMEM, VMEM],
        out_specs=(VMEM, VMEM, VMEM),
        compiler_params=params(),
        name="pack_blocks",
    )(rows, cols, dests, weight, one, two)


def backward_kernel(kept, ids, slices, *refs):
    count = len(ids)
    packs = refs[:count]
    up_ref = refs[count]
    shares = refs[count + 1 : count + 1 + slices]
    meta_ref = refs[count + 1 + slices]
    acc, meta_s, sem = refs[count + 2 + slices :]
    side = packs[0].shape[1]
    pitch = side + TILE
    width = shares[0].shape[1]
    for at, ident in enumerate(ids):
        for s in range(kept):
            tile = packs[at][s * pitch + side : (s + 1) * pitch, :].astype(f32)
            row = ident * kept + s
            meta_ref[row : row + 1, :] = tile[0:1, :].astype(jnp.int32)
    copy = pltpu.make_async_copy(meta_ref, meta_s, sem)
    copy.start()
    acc[...] = jnp.zeros_like(acc)
    copy.wait()
    for at, ident in enumerate(ids):
        for s in range(kept):
            row = meta_s[ident * kept + s, 0]
            col = meta_s[ident * kept + s, 1]
            part = lax.dot_general(
                lanes(up_ref, col, side),
                packs[at][s * pitch : s * pitch + side, :],
                (((1,), (1,)), ((), ())),
                preferred_element_type=f32,
            )
            place = pl.ds(pl.multiple_of(row * side, side), side)
            acc[:, place] = acc[:, place] + part
    me = lax.axis_index("mp")
    for k in range(slices):
        share = lanes(acc, lax.rem(me + k, slices), width) * grad_scale
        shares[k][...] = share.astype(shares[k].dtype)


def backward(packs, ids, upstream, kept, slices, features):
    tokens = upstream.shape[0]
    side = packs[0].shape[1]
    blocks = len(ids) * kept
    shares = [
        jax.ShapeDtypeStruct((tokens, features), f32 if k == 0 else bf16) for k in range(slices)
    ]
    outs = pl.pallas_call(
        functools.partial(backward_kernel, kept, ids, slices),
        out_shape=(*shares, jax.ShapeDtypeStruct((blocks, side), jnp.int32)),
        in_specs=[VMEM] * (len(ids) + 1),
        out_specs=(VMEM,) * (slices + 1),
        scratch_shapes=[
            pltpu.VMEM((tokens, slices * features), f32),
            pltpu.SMEM((blocks, side), jnp.int32),
            pltpu.SemaphoreType.DMA,
        ],
        compiler_params=params(),
        cost_estimate=pl.CostEstimate(
            flops=2 * blocks * tokens * side * side,
            bytes_accessed=24 * 1024 * 1024,
            transcendentals=0,
        ),
        name="input_gradient",
    )(*packs, upstream)
    return outs[:slices], outs[slices]


def line_reduce(shares, axis):
    n = len(shares)
    right = left = None
    for step in range(1, n):
        to_right, to_left = shares[n - step], shares[step]
        if right is not None:
            to_right = (to_right.astype(f32) + right.astype(f32)).astype(bf16)
            to_left = (to_left.astype(f32) + left.astype(f32)).astype(bf16)
        right = lax.ppermute(to_right, axis, [(i, i + 1) for i in range(step)])
        left = lax.ppermute(to_left, axis, [(n - 1 - i, n - 2 - i) for i in range(step)])
    if right is None:
        return shares[0].astype(bf16)
    return (shares[0] + right.astype(f32) + left.astype(f32)).astype(bf16)


def gradient_kernel(kept, dp, meta_s, x_ref, up_ref, keep_ref, send_ref, store):
    side = keep_ref.shape[1]
    per = x_ref.shape[2] // side
    blocks = dp * kept
    bits = dp.bit_length() - 1
    me = lax.axis_index("dp")
    store[0:blocks] = jnp.zeros((blocks, side, side), f32)
    for b in range(blocks):
        row, col, dest = meta_s[b, 0], meta_s[b, 1], meta_s[b, 2]
        x = x_ref[row // per, :, pl.ds(pl.multiple_of((row % per) * side, side), side)]
        grad = lax.dot_general(
            x, lanes(up_ref, col, side), (((0,), (0,)), ((), ())), preferred_element_type=f32
        )
        gap = jnp.bitwise_xor(jnp.maximum(dest, 0) // kept, me)
        place = jnp.int32(0)
        for bit in range(bits):
            place = place * 2 + (lax.shift_right_logical(gap, bit) & 1)
        slot = jnp.where(dest >= 0, place * kept + jnp.maximum(dest, 0) % kept, blocks)
        store[slot] = grad * grad_scale
    half = keep_ref.shape[0]
    keep_ref[...] = store[0:half]
    send_ref[...] = store[half : 2 * half].astype(bf16)


def gradient(meta, x_all, upstream, kept, dp):
    side = meta.shape[1]
    blocks = dp * kept
    half = blocks // 2
    return pl.pallas_call(
        functools.partial(gradient_kernel, kept, dp),
        out_shape=(
            jax.ShapeDtypeStruct((half, side, side), f32),
            jax.ShapeDtypeStruct((half, side, side), bf16),
        ),
        in_specs=[SMEM, VMEM, VMEM],
        out_specs=(VMEM, VMEM),
        scratch_shapes=[pltpu.VMEM((blocks + 1, side, side), f32)],
        compiler_params=params(),
        cost_estimate=pl.CostEstimate(
            flops=2 * blocks * upstream.shape[0] * side * side,
            bytes_accessed=16 * 1024 * 1024,
            transcendentals=0,
        ),
        name="weight_gradient",
    )(meta, x_all, upstream)


def halving_reduce(keep, send, dp):
    step = 1
    while True:
        came = lax.ppermute(send, "dp", [(i, i ^ step) for i in range(dp)])
        step *= 2
        if step == dp:
            return keep, came
        total = keep + came.astype(f32)
        half = total.shape[0] // 2
        keep, send = total[:half], total[half:].astype(bf16)


def forward_kernel(kept, ids, meta_s, *refs):
    count = len(ids)
    packs = refs[:count]
    x_ref, out_ref, acc = refs[count:]
    side = packs[0].shape[1]
    pitch = side + TILE
    per = x_ref.shape[2] // side
    acc[...] = jnp.zeros_like(acc)
    for at, ident in enumerate(ids):
        for s in range(kept):
            row = meta_s[ident * kept + s, 0]
            col = meta_s[ident * kept + s, 1]
            x = x_ref[row // per, :, pl.ds(pl.multiple_of((row % per) * side, side), side)]
            part = jnp.dot(
                x, packs[at][s * pitch : s * pitch + side, :], preferred_element_type=f32
            )
            place = pl.ds(pl.multiple_of(col * side, side), side)
            acc[:, place] = acc[:, place] + part
    out_ref[...] = (acc[...] * grad_scale).astype(bf16)


def forward(meta, packs, ids, x_all, kept, hidden):
    tokens = x_all.shape[1]
    side = meta.shape[1]
    return pl.pallas_call(
        functools.partial(forward_kernel, kept, ids),
        out_shape=jax.ShapeDtypeStruct((tokens, hidden), bf16),
        in_specs=[SMEM] + [VMEM] * (len(ids) + 1),
        out_specs=VMEM,
        scratch_shapes=[pltpu.VMEM((tokens, hidden), f32)],
        compiler_params=params(),
        cost_estimate=pl.CostEstimate(
            flops=2 * len(ids) * kept * tokens * side * side,
            bytes_accessed=24 * 1024 * 1024,
            transcendentals=0,
        ),
        name="hidden_out",
    )(meta, *packs, x_all)


def update_kernel(
    dp, meta_s, keep_ref, came_ref, w_ref, one_ref, two_ref, left_ref, right_ref,
    new_w, new_one, new_two,
):
    kept, side = w_ref.shape[0], w_ref.shape[1]
    travel = 3 * side
    me = lax.axis_index("dp")
    source = [jnp.int32(-1)] * kept

    def place(source, dest, here, code):
        mine = here & (dest >= 0) & (jnp.maximum(dest, 0) // kept == me)
        slot = jnp.maximum(dest, 0) % kept
        found = [jnp.where(mine & (slot == q), code, source[q]) for q in range(kept)]
        return found, code + mine.astype(jnp.int32)

    for s in range(kept):
        source, _ = place(source, meta_s[s, 2], True, jnp.int32(s))
    for side_at, other in ((kept, me - 1), (kept + kept // 2, me + 1)):
        here = (other >= 0) & (other < dp)
        gap = jnp.where(here, jnp.bitwise_xor(jnp.clip(other, 0, dp - 1), me), 0)
        code = jnp.int32(side_at)
        for s in range(kept):
            source, code = place(source, meta_s[gap * kept + s, 2], here, code)

    for q in range(kept):

        def write(weight, one, two, q=q):
            grad = keep_ref[q] + came_ref[q].astype(f32)
            first = beta_first * one + (1.0 - beta_first) * grad
            second = beta_second * two + (1.0 - beta_second) * grad * grad
            stepped = weight - learn_rate * first / (jnp.sqrt(second) + epsilon)
            new_w[q] = stepped.astype(bf16)
            new_one[q] = first
            new_two[q] = second

        @pl.when(source[q] < 0)
        def _(q=q):
            new_w[q] = jnp.zeros((side, side), bf16)
            new_one[q] = jnp.zeros((side, side), f32)
            new_two[q] = jnp.zeros((side, side), f32)

        @pl.when((source[q] >= 0) & (source[q] < kept))
        def _(q=q):
            s = jnp.clip(source[q], 0, kept - 1)
            write(w_ref[s].astype(f32), one_ref[s], two_ref[s])

        for ref, first_code in ((left_ref, kept), (right_ref, kept + kept // 2)):

            @pl.when((source[q] >= first_code) & (source[q] < first_code + kept // 2))
            def _(q=q, ref=ref, first_code=first_code):
                rank = jnp.clip(source[q] - first_code, 0, kept // 2 - 1)
                base = pl.multiple_of(rank * travel, TILE)
                write(
                    ref[pl.ds(base, side), :].astype(f32),
                    ref[pl.ds(base + side, side), :].astype(f32),
                    ref[pl.ds(base + 2 * side, side), :].astype(f32),
                )


def update(meta, keep, came, weight, one, two, from_left, from_right, dp):
    shape = weight.shape
    return pl.pallas_call(
        functools.partial(update_kernel, dp),
        out_shape=(
            jax.ShapeDtypeStruct(shape, bf16),
            jax.ShapeDtypeStruct(shape, f32),
            jax.ShapeDtypeStruct(shape, f32),
        ),
        in_specs=[SMEM] + [VMEM] * 7,
        out_specs=(VMEM,) * 3,
        compiler_params=params(),
        name="adam_update",
    )(meta, keep, came, weight, one, two, from_left, from_right)


def body(weight, moment_one, moment_two, block_row, block_col, dest_slot, tokens, upstream):
    kept = weight.shape[0]
    dp = lax.axis_size("dp")
    slices = lax.axis_size("mp")
    x_all = lax.all_gather(tokens, "mp", axis=0)
    packed, to_left, to_right = pack(
        block_row, block_col, dest_slot, weight, moment_one, moment_two
    )
    packs, ids = [packed], [0]
    bit = dp // 2
    while bit:
        packs = packs + [
            lax.ppermute(p, "dp", [(i, i ^ bit) for i in range(dp)]) for p in packs
        ]
        ids = ids + [i ^ bit for i in ids]
        bit //= 2
    from_left = lax.ppermute(to_right, "dp", [(i, i + 1) for i in range(dp - 1)])
    from_right = lax.ppermute(to_left, "dp", [(i + 1, i) for i in range(dp - 1)])
    ids = tuple(ids)
    shares, meta = backward(packs, ids, upstream, kept, slices, tokens.shape[1])
    input_grad = line_reduce(shares, "mp")
    keep, send = gradient(meta, x_all, upstream, kept, dp)
    hidden_out = forward(meta, packs, ids, x_all, kept, upstream.shape[1])
    keep, came = halving_reduce(keep, send, dp)
    new_weight, new_first, new_second = update(
        meta, keep, came, weight, moment_one, moment_two, from_left, from_right, dp
    )
    return (new_weight, new_first, new_second, hidden_out, input_grad)


def solution(mesh):
    blocks = P(("dp", "mp"), None, None)
    ints = P(("dp", "mp"))
    acts = P("dp", "mp")
    return jax.shard_map(
        body,
        mesh=mesh,
        in_specs=(blocks, blocks, blocks, ints, ints, ints, acts, acts),
        out_specs=(blocks, blocks, blocks, acts, acts),
        check_vma=False,
    )
```

```python
import functools
import math

import jax
import jax.numpy as jnp
from jax import lax
from jax.experimental import pallas as pl
from jax.experimental.pallas import tpu as pltpu
from jax.sharding import PartitionSpec as P

D = 8192
TILE = 16

learn_rate = 0.02
beta_first = 0.9
beta_second = 0.95
epsilon = 1e-08
grad_scale = 1.0 / math.sqrt(D)

f32 = jnp.float32
bf16 = jnp.bfloat16
VMEM = pl.BlockSpec(memory_space=pltpu.VMEM)
ANY = pl.BlockSpec(memory_space=pl.ANY)
SMEM = pl.BlockSpec(memory_space=pltpu.SMEM)


def params(mib=32):
    return pltpu.CompilerParams(vmem_limit_bytes=mib * 1024 * 1024)


def lanes(ref, index, width):
    return ref[:, pl.ds(pl.multiple_of(index * width, width), width)]


def pack_kernel(row_h, col_h, dest_h, w_h, pack_ref, row_s, col_s, dest_s, w_ref, sems):
    kept, side = w_ref.shape[0], w_ref.shape[1]
    pitch = side + TILE
    copies = [
        pltpu.make_async_copy(source, target, sems.at[i])
        for i, (source, target) in enumerate(
            ((row_h, row_s), (col_h, col_s), (dest_h, dest_s), (w_h, w_ref))
        )
    ]
    for copy in copies:
        copy.start()
    for copy in copies:
        copy.wait()
    lane = lax.broadcasted_iota(jnp.int32, (TILE, side), 1)
    for s in range(kept):
        tile = jnp.where(lane == 0, row_s[s], jnp.where(lane == 1, col_s[s], dest_s[s]))
        pack_ref[s * pitch : s * pitch + side, :] = w_ref[s]
        pack_ref[s * pitch + side : (s + 1) * pitch, :] = tile.astype(f32).astype(bf16)


def pack(rows, cols, dests, weight):
    kept, side, _ = weight.shape
    return pl.pallas_call(
        pack_kernel,
        out_shape=jax.ShapeDtypeStruct((kept * (side + TILE), side), bf16),
        in_specs=[ANY] * 4,
        out_specs=VMEM,
        scratch_shapes=[pltpu.SMEM((kept,), jnp.int32)] * 3
        + [pltpu.VMEM(weight.shape, bf16), pltpu.SemaphoreType.DMA((4,))],
        compiler_params=params(60),
        cost_estimate=pl.CostEstimate(flops=0, bytes_accessed=0, transcendentals=0),
        name="pack_blocks",
    )(rows, cols, dests, weight)


def leave_kernel(dest_h, w_h, one_h, two_h, left_ref, right_ref, dest_s, w_ref, one_ref, two_ref, sems):
    kept, side = w_ref.shape[0], w_ref.shape[1]
    half = kept // 2
    me = lax.axis_index("dp")
    travel = 3 * side
    copies = [
        pltpu.make_async_copy(source, target, sems.at[i])
        for i, (source, target) in enumerate(
            ((dest_h, dest_s), (w_h, w_ref), (one_h, one_ref), (two_h, two_ref))
        )
    ]
    for copy in copies:
        copy.start()
    left_ref[...] = jnp.zeros_like(left_ref)
    right_ref[...] = jnp.zeros_like(right_ref)
    for copy in copies:
        copy.wait()
    to_left = jnp.int32(0)
    to_right = jnp.int32(0)
    for s in range(kept):
        dest = dest_s[s]
        goal = jnp.where(dest >= 0, dest // kept, me)
        for ref, count, going in (
            (left_ref, to_left, goal < me),
            (right_ref, to_right, goal > me),
        ):

            @pl.when(going)
            def _(ref=ref, count=count, s=s):
                base = pl.multiple_of(jnp.minimum(count, half - 1) * travel, TILE)
                ref[pl.ds(base, side), :] = w_ref[s]
                ref[pl.ds(base + side, side), :] = one_ref[s].astype(bf16)
                ref[pl.ds(base + 2 * side, side), :] = two_ref[s].astype(bf16)

        to_left = to_left + (goal < me).astype(jnp.int32)
        to_right = to_right + (goal > me).astype(jnp.int32)


def leave(dests, weight, one, two):
    kept, side, _ = weight.shape
    travel = jax.ShapeDtypeStruct((kept // 2 * 3 * side, side), bf16)
    return pl.pallas_call(
        leave_kernel,
        out_shape=(travel, travel),
        in_specs=[ANY] * 4,
        out_specs=(VMEM, VMEM),
        scratch_shapes=[
            pltpu.SMEM((kept,), jnp.int32),
            pltpu.VMEM(weight.shape, bf16),
            pltpu.VMEM(weight.shape, f32),
            pltpu.VMEM(weight.shape, f32),
            pltpu.SemaphoreType.DMA((4,)),
        ],
        compiler_params=params(8),
        cost_estimate=pl.CostEstimate(flops=0, bytes_accessed=0, transcendentals=0),
        name="leaving_blocks",
    )(dests, weight, one, two)


def line_gather(own, axis):
    n = lax.axis_size(axis)
    below, above = [own], [own]
    for step in range(1, n):
        below.append(lax.ppermute(below[-1], axis, [(i, i + 1) for i in range(step - 1, n - 1)]))
        above.append(lax.ppermute(above[-1], axis, [(i + 1, i) for i in range(n - step)]))
    return (*below[1:], *above[1:])


def backward_kernel(kept, ids, slices, *refs):
    count = len(ids)
    packs, up_ref = refs[:count], refs[count]
    shares = refs[count + 1 : count + 1 + slices]
    meta_ref = refs[count + 1 + slices]
    acc, meta_s, sem = refs[count + 2 + slices :]
    side = meta_ref.shape[1]
    pitch = side + TILE
    width = shares[0].shape[1]
    for at, ident in enumerate(ids):
        for s in range(kept):
            tile = packs[at][s * pitch + side : (s + 1) * pitch, :].astype(f32)
            row = ident * kept + s
            meta_ref[row : row + 1, :] = tile[0:1, :].astype(jnp.int32)
    copy = pltpu.make_async_copy(meta_ref, meta_s, sem)
    copy.start()
    acc[...] = jnp.zeros_like(acc)
    copy.wait()
    for at, ident in enumerate(ids):
        for s in range(kept):
            row = meta_s[ident * kept + s, 0]
            col = meta_s[ident * kept + s, 1]
            part = lax.dot_general(
                lanes(up_ref, col, side),
                packs[at][s * pitch : s * pitch + side, :],
                (((1,), (1,)), ((), ())),
                preferred_element_type=f32,
            )
            place = pl.ds(pl.multiple_of(row * side, side), side)
            acc[:, place] = acc[:, place] + part
    for k, quarter in enumerate(share_order(lax.axis_index("mp"), slices)):
        share = lanes(acc, quarter, width) * grad_scale
        shares[k][...] = share.astype(shares[k].dtype)


def share_order(me, slices):
    if slices == 4:
        low = me < 2
        return (me, jnp.where(low, 3, 0), jnp.where(low, 2, 1), jnp.bitwise_xor(me, 1))
    return tuple(lax.rem(me + k, slices) for k in range(slices))


def backward(packs, ids, upstream, kept, slices, features):
    tokens = upstream.shape[0]
    side = packs[0].shape[1]
    blocks = len(ids) * kept
    shares = [
        jax.ShapeDtypeStruct((tokens, features), f32 if k == 0 else bf16) for k in range(slices)
    ]
    outs = pl.pallas_call(
        functools.partial(backward_kernel, kept, ids, slices),
        out_shape=(*shares, jax.ShapeDtypeStruct((blocks, side), jnp.int32)),
        in_specs=[VMEM] * (len(ids) + 1),
        out_specs=(VMEM,) * (slices + 1),
        scratch_shapes=[
            pltpu.VMEM((tokens, slices * features), f32),
            pltpu.SMEM((blocks, side), jnp.int32),
            pltpu.SemaphoreType.DMA,
        ],
        compiler_params=params(),
        cost_estimate=pl.CostEstimate(flops=0, bytes_accessed=0, transcendentals=0),
        name="input_gradient",
    )(*packs, upstream)
    return outs[:slices], outs[slices]


def line_reduce(shares, axis):
    n = len(shares)
    right = left = None
    for step in range(1, n):
        to_right, to_left = shares[n - step], shares[step]
        if right is not None:
            to_right = (to_right.astype(f32) + right.astype(f32)).astype(bf16)
            to_left = (to_left.astype(f32) + left.astype(f32)).astype(bf16)
        right = lax.ppermute(to_right, axis, [(i, i + 1) for i in range(step)])
        left = lax.ppermute(to_left, axis, [(n - 1 - i, n - 2 - i) for i in range(step)])
    if right is None:
        return shares[0].astype(bf16)
    return (shares[0] + right.astype(f32) + left.astype(f32)).astype(bf16)


def four_gather(own, axis):
    inner, outward = [(1, 2), (2, 1)], [(1, 0), (2, 3)]
    near = lax.ppermute(own, axis, [(0, 1), (1, 0), (2, 3), (3, 2)])
    middle = lax.ppermute(own, axis, inner)
    near, middle = lax.optimization_barrier((near, middle))
    near_on = lax.ppermute(near, axis, inner)
    middle_on = lax.ppermute(middle, axis, outward)
    near_on, middle_on = lax.optimization_barrier((near_on, middle_on))
    last = lax.ppermute(near_on, axis, outward)
    return near, middle, near_on, middle_on, last


def after(value, *others):
    return lax.optimization_barrier((value, *others))[0]


def plus(share, came):
    return (share.astype(f32) + came.astype(f32)).astype(bf16)


def token_copies(slices, own, came, x_ref, sems):
    me = lax.axis_index("mp")
    todo = [(None, own, me)]
    if slices == 4:
        near, middle, near_on, middle_on, last = came
        outer = lax.rem(me, 3) == 0
        todo.append((None, near, jnp.bitwise_xor(me, 1)))
        todo.append((outer, middle_on, jnp.where(me == 0, 2, 1)))
        todo.append((outer, last, 3 - me))
        todo.append((jnp.logical_not(outer), middle, 3 - me))
        todo.append((jnp.logical_not(outer), near_on, jnp.where(me == 1, 3, 0)))
    else:
        for k in range(1, slices):
            todo.append((me >= k, came[k - 1], jnp.maximum(me - k, 0)))
            todo.append((me + k < slices, came[slices + k - 2], jnp.minimum(me + k, slices - 1)))
    return [
        (when, pltpu.make_async_copy(source, x_ref.at[at], sems.at[i]))
        for i, (when, source, at) in enumerate(todo)
    ]


def run(when, action):
    if when is None:
        action()
    else:
        pl.when(when)(action)


def gradient_kernel(kept, dp, slices, meta_s, up_h, own_h, *refs):
    came, (keep_ref, send_ref, x_ref, up_ref, store, sems) = refs[:-6], refs[-6:]
    side = keep_ref.shape[1]
    per = x_ref.shape[2] // side
    blocks = dp * kept
    me = lax.axis_index("dp")
    up_copy = pltpu.make_async_copy(up_h, up_ref, sems.at[len(came) + 1])
    copies = token_copies(slices, own_h, came, x_ref, sems)
    up_copy.start()
    for when, copy in copies:
        run(when, copy.start)
    store[0:blocks] = jnp.zeros((blocks, side, side), f32)
    up_copy.wait()
    for when, copy in copies:
        run(when, copy.wait)
    for b in range(blocks):
        row, col, dest = meta_s[b, 0], meta_s[b, 1], meta_s[b, 2]
        x = x_ref[row // per, :, pl.ds(pl.multiple_of((row % per) * side, side), side)]
        grad = lax.dot_general(
            x, lanes(up_ref, col, side), (((0,), (0,)), ((), ())), preferred_element_type=f32
        )
        gap = jnp.bitwise_xor(jnp.maximum(dest, 0) // kept, me)
        place = (gap & 1) * (dp // 2) + lax.shift_right_logical(gap, 1)
        slot = jnp.where(dest >= 0, place * kept + jnp.maximum(dest, 0) % kept, blocks)
        store[slot] = grad * grad_scale
    half = keep_ref.shape[0]
    keep_ref[...] = store[0:half]
    send_ref[...] = store[half : 2 * half].astype(bf16)


def gradient(meta, own, came, upstream, kept, dp, slices):
    side = meta.shape[1]
    blocks = dp * kept
    half = blocks // 2
    return pl.pallas_call(
        functools.partial(gradient_kernel, kept, dp, slices),
        out_shape=(
            jax.ShapeDtypeStruct((half, side, side), f32),
            jax.ShapeDtypeStruct((half, side, side), bf16),
        ),
        in_specs=[SMEM] + [ANY] * (2 + len(came)),
        out_specs=(VMEM, VMEM),
        scratch_shapes=[
            pltpu.VMEM((slices, *own.shape), bf16),
            pltpu.VMEM(upstream.shape, bf16),
            pltpu.VMEM((blocks + 1, side, side), f32),
            pltpu.SemaphoreType.DMA((len(came) + 2,)),
        ],
        compiler_params=params(),
        cost_estimate=pl.CostEstimate(flops=0, bytes_accessed=0, transcendentals=0),
        name="weight_gradient",
    )(meta, upstream, own, *came)


def slot_reduce(keep, send, kept, dp):
    came = lax.ppermute(send, "dp", [(i, i ^ 1) for i in range(dp)])
    total = keep + came.astype(f32)
    totals = [total[:kept]]
    for gap in range(1, dp // 2):
        totals.append(total[gap * kept : (gap + 1) * kept].astype(bf16))
    parts = totals[:1]
    for gap in range(1, dp // 2):
        parts.append(lax.ppermute(totals[gap], "dp", [(i, i ^ (2 * gap)) for i in range(dp)]))
    return parts, totals


def forward_kernel(kept, ids, slices, meta_s, *refs):
    count = len(ids)
    packs, own_h, came = refs[:count], refs[count], refs[count + 1 : -4]
    out_ref, x_ref, acc, sems = refs[-4:]
    side = packs[0].shape[1]
    pitch = side + TILE
    per = x_ref.shape[2] // side
    copies = token_copies(slices, own_h, came, x_ref, sems)
    for when, copy in copies:
        run(when, copy.start)
    acc[...] = jnp.zeros_like(acc)
    for when, copy in copies:
        run(when, copy.wait)
    for at, ident in enumerate(ids):
        for s in range(kept):
            row = meta_s[ident * kept + s, 0]
            col = meta_s[ident * kept + s, 1]
            x = x_ref[row // per, :, pl.ds(pl.multiple_of((row % per) * side, side), side)]
            part = jnp.dot(
                x, packs[at][s * pitch : s * pitch + side, :], preferred_element_type=f32
            )
            place = pl.ds(pl.multiple_of(col * side, side), side)
            acc[:, place] = acc[:, place] + part
    out_ref[...] = (acc[...] * grad_scale).astype(bf16)


def forward(meta, packs, ids, own, came, kept, slices, hidden):
    tokens = own.shape[0]
    side = meta.shape[1]
    return pl.pallas_call(
        functools.partial(forward_kernel, kept, ids, slices),
        out_shape=jax.ShapeDtypeStruct((tokens, hidden), bf16),
        in_specs=[SMEM] + [VMEM] * len(ids) + [ANY] * (1 + len(came)),
        out_specs=VMEM,
        scratch_shapes=[
            pltpu.VMEM((slices, *own.shape), bf16),
            pltpu.VMEM((tokens, hidden), f32),
            pltpu.SemaphoreType.DMA((len(came) + 1,)),
        ],
        compiler_params=params(),
        cost_estimate=pl.CostEstimate(flops=0, bytes_accessed=0, transcendentals=0),
        name="hidden_out",
    )(meta, *packs, own, *came)


def update_kernel(
    dp, meta_s, w_ref, one_ref, two_ref, left_ref, right_ref, *refs
):
    parts, (new_w, new_one, new_two) = refs[:-3], refs[-3:]
    kept, side = w_ref.shape[0], w_ref.shape[1]
    travel = 3 * side
    me = lax.axis_index("dp")
    source = [jnp.int32(-1)] * kept

    def place(source, dest, here, code):
        mine = here & (dest >= 0) & (jnp.maximum(dest, 0) // kept == me)
        slot = jnp.maximum(dest, 0) % kept
        found = [jnp.where(mine & (slot == q), code, source[q]) for q in range(kept)]
        return found, code + mine.astype(jnp.int32)

    for s in range(kept):
        source, _ = place(source, meta_s[s, 2], True, jnp.int32(s))
    for side_at, other in ((kept, me - 1), (kept + kept // 2, me + 1)):
        here = (other >= 0) & (other < dp)
        gap = jnp.where(here, jnp.bitwise_xor(jnp.clip(other, 0, dp - 1), me), 0)
        code = jnp.int32(side_at)
        for s in range(kept):
            source, code = place(source, meta_s[gap * kept + s, 2], here, code)

    for q in range(kept):

        def write(weight, one, two, q=q):
            grad = parts[0][q]
            for part in parts[1:]:
                grad = grad + part[q].astype(f32)
            first = beta_first * one + (1.0 - beta_first) * grad
            second = beta_second * two + (1.0 - beta_second) * grad * grad
            stepped = weight - learn_rate * first / (jnp.sqrt(second) + epsilon)
            new_w[q] = stepped.astype(bf16)
            new_one[q] = first
            new_two[q] = second

        @pl.when(source[q] < 0)
        def _(q=q):
            new_w[q] = jnp.zeros((side, side), bf16)
            new_one[q] = jnp.zeros((side, side), f32)
            new_two[q] = jnp.zeros((side, side), f32)

        @pl.when((source[q] >= 0) & (source[q] < kept))
        def _(q=q):
            s = jnp.clip(source[q], 0, kept - 1)
            write(w_ref[s].astype(f32), one_ref[s], two_ref[s])

        for ref, first_code in ((left_ref, kept), (right_ref, kept + kept // 2)):

            @pl.when((source[q] >= first_code) & (source[q] < first_code + kept // 2))
            def _(q=q, ref=ref, first_code=first_code):
                rank = jnp.clip(source[q] - first_code, 0, kept // 2 - 1)
                base = pl.multiple_of(rank * travel, TILE)
                write(
                    ref[pl.ds(base, side), :].astype(f32),
                    ref[pl.ds(base + side, side), :].astype(f32),
                    ref[pl.ds(base + 2 * side, side), :].astype(f32),
                )


def update(meta, parts, weight, one, two, from_left, from_right, dp):
    shape = weight.shape
    return pl.pallas_call(
        functools.partial(update_kernel, dp),
        out_shape=(
            jax.ShapeDtypeStruct(shape, bf16),
            jax.ShapeDtypeStruct(shape, f32),
            jax.ShapeDtypeStruct(shape, f32),
        ),
        in_specs=[SMEM] + [VMEM] * (5 + len(parts)),
        out_specs=(VMEM,) * 3,
        compiler_params=params(),
        cost_estimate=pl.CostEstimate(flops=0, bytes_accessed=0, transcendentals=0),
        name="adam_update",
    )(meta, weight, one, two, from_left, from_right, *parts)


def body(weight, moment_one, moment_two, block_row, block_col, dest_slot, tokens, upstream):
    kept = weight.shape[0]
    dp = lax.axis_size("dp")
    slices = lax.axis_size("mp")
    four = slices == 4
    came = four_gather(tokens, "mp") if four else line_gather(tokens, "mp")
    packs, ids = [pack(block_row, block_col, dest_slot, weight)], [0]
    bit = dp // 2
    while bit:
        packs = packs + [
            lax.ppermute(p, "dp", [(i, i ^ bit) for i in range(dp)]) for p in packs
        ]
        ids = ids + [i ^ bit for i in ids]
        bit //= 2
    ids = tuple(ids)
    if four:
        packs[-1] = after(packs[-1], came[0], came[1])
    shares, meta = backward(packs, ids, upstream, kept, slices, tokens.shape[1])
    if four:
        own, far, second, near = shares
        ends, inner = [(0, 1), (3, 2)], [(1, 2), (2, 1)]
        came_far = lax.ppermute(far, "mp", ends)
        dest_leave = after(dest_slot, meta, came[2])
    else:
        dest_leave = dest_slot
    to_left, to_right = leave(dest_leave, weight, moment_one, moment_two)
    from_left = lax.ppermute(to_right, "dp", [(i, i + 1) for i in range(dp - 1)])
    from_right = lax.ppermute(to_left, "dp", [(i + 1, i) for i in range(dp - 1)])
    if four:
        sum_far = plus(after(far, from_left, from_right), came_far)
        passed_far = lax.ppermute(sum_far, "mp", inner)
        came_second = lax.ppermute(after(second, sum_far), "mp", ends)
        meta_grad = after(meta, sum_far)
    else:
        meta_grad = meta
    keep, send = gradient(meta_grad, tokens, came, upstream, kept, dp, slices)
    parts, totals = slot_reduce(keep, send, kept, dp)
    if four:
        passed_far, came_second = lax.optimization_barrier((passed_far, came_second))
        sum_second = plus(after(second, *totals), came_second)
        sum_near = plus(near, passed_far)
        sum_second, sum_near = lax.optimization_barrier((sum_second, sum_near))
        passed_second = lax.ppermute(sum_second, "mp", inner)
        came_near = lax.ppermute(sum_near, "mp", ends + [(1, 0), (2, 3)])
        meta_out = after(meta, sum_second, sum_near)
        input_grad = (own + came_near.astype(f32) + passed_second.astype(f32)).astype(bf16)
    else:
        meta_out = meta
        input_grad = line_reduce(shares, "mp")
    hidden_out = forward(
        meta_out, packs, ids, tokens, came, kept, slices, upstream.shape[1]
    )
    new_weight, new_first, new_second = update(
        meta, parts, weight, moment_one, moment_two, from_left, from_right, dp
    )
    return (new_weight, new_first, new_second, hidden_out, input_grad)


def solution(mesh):
    blocks = P(("dp", "mp"), None, None)
    ints = P(("dp", "mp"))
    acts = P("dp", "mp")
    return jax.shard_map(
        body,
        mesh=mesh,
        in_specs=(blocks, blocks, blocks, ints, ints, ints, acts, acts),
        out_specs=(blocks, blocks, blocks, acts, acts),
        check_vma=False,
    )
```

```python
import functools
import math

import jax
import jax.numpy as jnp
from jax import lax
from jax.experimental import pallas as pl
from jax.experimental.pallas import tpu as pltpu
from jax.sharding import PartitionSpec as P

D = 8192
TILE = 16

learn_rate = 0.02
beta_first = 0.9
beta_second = 0.95
epsilon = 1e-08
grad_scale = 1.0 / math.sqrt(D)

f32 = jnp.float32
bf16 = jnp.bfloat16
VMEM = pl.BlockSpec(memory_space=pltpu.VMEM)
ANY = pl.BlockSpec(memory_space=pl.ANY)
SMEM = pl.BlockSpec(memory_space=pltpu.SMEM)
HBM = pl.BlockSpec(memory_space=pltpu.HBM)


def params(mib=24):
    return pltpu.CompilerParams(vmem_limit_bytes=mib * 1024 * 1024)


def lanes(ref, index, width):
    return ref[:, pl.ds(pl.multiple_of(index * width, width), width)]


def pack_kernel(row_h, col_h, dest_h, w_h, pack_ref, row_s, col_s, dest_s, w_ref, sems):
    kept, side = w_ref.shape[0], w_ref.shape[1]
    pitch = side + TILE
    copies = [
        pltpu.make_async_copy(source, target, sems.at[i])
        for i, (source, target) in enumerate(
            ((row_h, row_s), (col_h, col_s), (dest_h, dest_s), (w_h, w_ref))
        )
    ]
    for copy in copies:
        copy.start()
    for copy in copies:
        copy.wait()
    lane = lax.broadcasted_iota(jnp.int32, (TILE, side), 1)
    for s in range(kept):
        tile = jnp.where(lane == 0, row_s[s], jnp.where(lane == 1, col_s[s], dest_s[s]))
        pack_ref[s * pitch : s * pitch + side, :] = w_ref[s]
        pack_ref[s * pitch + side : (s + 1) * pitch, :] = tile.astype(f32).astype(bf16)


def pack(rows, cols, dests, weight):
    kept, side, _ = weight.shape
    return pl.pallas_call(
        pack_kernel,
        out_shape=jax.ShapeDtypeStruct((kept * (side + TILE), side), bf16),
        in_specs=[ANY] * 4,
        out_specs=VMEM,
        scratch_shapes=[pltpu.SMEM((kept,), jnp.int32)] * 3
        + [pltpu.VMEM(weight.shape, bf16), pltpu.SemaphoreType.DMA((4,))],
        compiler_params=params(60),
        cost_estimate=pl.CostEstimate(flops=0, bytes_accessed=0, transcendentals=0),
        name="pack_blocks",
    )(rows, cols, dests, weight)


def hold_kernel(count, *refs):
    sems = refs[-1]
    copies = [
        pltpu.make_async_copy(refs[i], refs[count + i], sems.at[i]) for i in range(count)
    ]
    for copy in copies:
        copy.start()
    for copy in copies:
        copy.wait()


def hold(*arrays):
    count = len(arrays)
    return pl.pallas_call(
        functools.partial(hold_kernel, count),
        out_shape=tuple(jax.ShapeDtypeStruct(a.shape, a.dtype) for a in arrays),
        in_specs=[ANY] * count,
        out_specs=(VMEM,) * count,
        scratch_shapes=[pltpu.SemaphoreType.DMA((count,))],
        compiler_params=params(8),
        cost_estimate=pl.CostEstimate(flops=0, bytes_accessed=0, transcendentals=0),
        name="hold_arrays",
    )(*arrays)


def leave_kernel(dest_h, w_h, one_h, two_h, left_ref, right_ref, dest_s, w_ref, one_ref, two_ref, sems):
    kept, side = w_ref.shape[0], w_ref.shape[1]
    half = kept // 2
    me = lax.axis_index("dp")
    travel = 3 * side
    copies = [
        pltpu.make_async_copy(source, target, sems.at[i])
        for i, (source, target) in enumerate(
            ((dest_h, dest_s), (w_h, w_ref), (one_h, one_ref), (two_h, two_ref))
        )
    ]
    for copy in copies:
        copy.start()
    left_ref[...] = jnp.zeros_like(left_ref)
    right_ref[...] = jnp.zeros_like(right_ref)
    for copy in copies:
        copy.wait()
    to_left = jnp.int32(0)
    to_right = jnp.int32(0)
    for s in range(kept):
        dest = dest_s[s]
        goal = jnp.where(dest >= 0, dest // kept, me)
        for ref, count, going in (
            (left_ref, to_left, goal < me),
            (right_ref, to_right, goal > me),
        ):

            @pl.when(going)
            def _(ref=ref, count=count, s=s):
                base = pl.multiple_of(jnp.minimum(count, half - 1) * travel, TILE)
                ref[pl.ds(base, side), :] = w_ref[s]
                ref[pl.ds(base + side, side), :] = one_ref[s].astype(bf16)
                ref[pl.ds(base + 2 * side, side), :] = two_ref[s].astype(bf16)

        to_left = to_left + (goal < me).astype(jnp.int32)
        to_right = to_right + (goal > me).astype(jnp.int32)


def leave(dests, weight, one, two):
    kept, side, _ = weight.shape
    travel = jax.ShapeDtypeStruct((kept // 2 * 3 * side, side), bf16)
    return pl.pallas_call(
        leave_kernel,
        out_shape=(travel, travel),
        in_specs=[ANY] * 4,
        out_specs=(VMEM, VMEM),
        scratch_shapes=[
            pltpu.SMEM((kept,), jnp.int32),
            pltpu.VMEM(weight.shape, bf16),
            pltpu.VMEM(weight.shape, f32),
            pltpu.VMEM(weight.shape, f32),
            pltpu.SemaphoreType.DMA((4,)),
        ],
        compiler_params=params(8),
        cost_estimate=pl.CostEstimate(flops=0, bytes_accessed=0, transcendentals=0),
        name="leaving_blocks",
    )(dests, weight, one, two)


def line_gather(own, axis):
    n = lax.axis_size(axis)
    below, above = [own], [own]
    for step in range(1, n):
        below.append(lax.ppermute(below[-1], axis, [(i, i + 1) for i in range(step - 1, n - 1)]))
        above.append(lax.ppermute(above[-1], axis, [(i + 1, i) for i in range(n - step)]))
    return (*below[1:], *above[1:])


def backward_kernel(kept, ids, slices, *refs):
    count = len(ids)
    packs, up_ref = refs[:count], refs[count]
    acc, meta_s, *held, sems = refs[-3 - slices :]
    if slices == 4:
        middle_ref, refs = refs[count + 1], refs[count + 2 : -3 - slices]
        mix_ref = refs[slices + 1]
    else:
        refs = refs[count + 1 : -3 - slices]
    shares, meta_ref = refs[:slices], refs[slices]
    side = meta_ref.shape[1]
    pitch = side + TILE
    width = shares[0].shape[1]
    for at, ident in enumerate(ids):
        for s in range(kept):
            tile = packs[at][s * pitch + side : (s + 1) * pitch, :].astype(f32)
            row = ident * kept + s
            meta_ref[row : row + 1, :] = tile[0:1, :].astype(jnp.int32)
    copy = pltpu.make_async_copy(meta_ref, meta_s, sems.at[slices])
    copy.start()
    acc[...] = jnp.zeros_like(acc)
    copy.wait()
    for at, ident in enumerate(ids):
        for s in range(kept):
            row = meta_s[ident * kept + s, 0]
            col = meta_s[ident * kept + s, 1]
            part = lax.dot_general(
                lanes(up_ref, col, side),
                packs[at][s * pitch : s * pitch + side, :],
                (((1,), (1,)), ((), ())),
                preferred_element_type=f32,
            )
            place = pl.ds(pl.multiple_of(row * side, side), side)
            acc[:, place] = acc[:, place] + part
    order = share_order(lax.axis_index("mp"), slices)
    copies = [pltpu.make_async_copy(held[k], shares[k], sems.at[k]) for k in range(slices)]
    for k, quarter in enumerate(order):
        share = lanes(acc, quarter, width) * grad_scale
        held[k][...] = share.astype(held[k].dtype)
        copies[k].start()
    if slices == 4:
        outer = lax.rem(lax.axis_index("mp"), 3) == 0

        @pl.when(outer)
        def _():
            mix_ref[...] = held[1][...]

        @pl.when(jnp.logical_not(outer))
        def _():
            mix_ref[...] = middle_ref[...]

    for copy in copies:
        copy.wait()


def share_order(me, slices):
    if slices == 4:
        low = me < 2
        return (me, jnp.where(low, 3, 0), jnp.where(low, 2, 1), jnp.bitwise_xor(me, 1))
    return tuple(lax.rem(me + k, slices) for k in range(slices))


def backward(packs, ids, upstream, middle, kept, slices, features):
    tokens = upstream.shape[0]
    side = packs[0].shape[1]
    blocks = len(ids) * kept
    shares = [
        jax.ShapeDtypeStruct((tokens, features), f32 if k == 0 else bf16) for k in range(slices)
    ]
    mixed = [jax.ShapeDtypeStruct((tokens, features), bf16) for _ in middle]
    outs = pl.pallas_call(
        functools.partial(backward_kernel, kept, ids, slices),
        out_shape=(*shares, jax.ShapeDtypeStruct((blocks, side), jnp.int32), *mixed),
        in_specs=[VMEM] * (len(ids) + 1 + len(middle)),
        out_specs=(HBM,) * slices + (VMEM,) * (1 + len(mixed)),
        scratch_shapes=[
            pltpu.VMEM((tokens, slices * features), f32),
            pltpu.SMEM((blocks, side), jnp.int32),
            *(pltpu.VMEM(share.shape, share.dtype) for share in shares),
            pltpu.SemaphoreType.DMA((slices + 1,)),
        ],
        compiler_params=params(),
        cost_estimate=pl.CostEstimate(flops=0, bytes_accessed=0, transcendentals=0),
        name="input_gradient",
    )(*packs, upstream, *middle)
    return outs[:slices], outs[slices], outs[slices + 1 :]


def line_reduce(shares, axis):
    n = len(shares)
    right = left = None
    for step in range(1, n):
        to_right, to_left = shares[n - step], shares[step]
        if right is not None:
            to_right = (to_right.astype(f32) + right.astype(f32)).astype(bf16)
            to_left = (to_left.astype(f32) + left.astype(f32)).astype(bf16)
        right = lax.ppermute(to_right, axis, [(i, i + 1) for i in range(step)])
        left = lax.ppermute(to_left, axis, [(n - 1 - i, n - 2 - i) for i in range(step)])
    if right is None:
        return shares[0].astype(bf16)
    return (shares[0] + right.astype(f32) + left.astype(f32)).astype(bf16)


def after(value, *others):
    return lax.optimization_barrier((value, *others))[0]


def sum_kernel(far_h, came_h, sum_ref, far_ref, came_ref, sems):
    @pl.when(lax.rem(lax.axis_index("mp"), 3) != 0)
    def _():
        copies = [
            pltpu.make_async_copy(far_h, far_ref, sems.at[0]),
            pltpu.make_async_copy(came_h, came_ref, sems.at[1]),
        ]
        for copy in copies:
            copy.start()
        for copy in copies:
            copy.wait()
        sum_ref[...] = (far_ref[...].astype(f32) + came_ref[...].astype(f32)).astype(bf16)


def inner_sum(far, came):
    return pl.pallas_call(
        sum_kernel,
        out_shape=jax.ShapeDtypeStruct(far.shape, bf16),
        in_specs=[ANY] * 2,
        out_specs=VMEM,
        scratch_shapes=[
            pltpu.VMEM(far.shape, bf16),
            pltpu.VMEM(far.shape, bf16),
            pltpu.SemaphoreType.DMA((2,)),
        ],
        compiler_params=params(),
        cost_estimate=pl.CostEstimate(flops=0, bytes_accessed=0, transcendentals=0),
        name="inner_sum",
    )(far, came)


def choose_kernel(outer_h, inner_h, mixed_ref, sem):
    outer = lax.rem(lax.axis_index("mp"), 3) == 0
    for when, source in ((outer, outer_h), (jnp.logical_not(outer), inner_h)):

        @pl.when(when)
        def _(source=source):
            copy = pltpu.make_async_copy(source, mixed_ref, sem)
            copy.start()
            copy.wait()


def choose(at_outer, at_inner):
    return pl.pallas_call(
        choose_kernel,
        out_shape=jax.ShapeDtypeStruct(at_outer.shape, bf16),
        in_specs=[ANY] * 2,
        out_specs=VMEM,
        scratch_shapes=[pltpu.SemaphoreType.DMA],
        compiler_params=params(),
        cost_estimate=pl.CostEstimate(flops=0, bytes_accessed=0, transcendentals=0),
        name="choose_sent",
    )(at_outer, at_inner)


def plus(share, came):
    return (share.astype(f32) + came.astype(f32)).astype(bf16)


def token_copies(slices, own, came, x_ref, sems):
    me = lax.axis_index("mp")
    todo = [(None, own, me)]
    if slices == 4:
        near, middle, near_on, mixed, mixed_on = came
        outer = lax.rem(me, 3) == 0
        todo.append((None, near, jnp.bitwise_xor(me, 1)))
        todo.append((outer, mixed, jnp.where(me == 0, 2, 1)))
        todo.append((outer, mixed_on, 3 - me))
        todo.append((jnp.logical_not(outer), middle, 3 - me))
        todo.append((jnp.logical_not(outer), near_on, jnp.where(me == 1, 3, 0)))
    else:
        for k in range(1, slices):
            todo.append((me >= k, came[k - 1], jnp.maximum(me - k, 0)))
            todo.append((me + k < slices, came[slices + k - 2], jnp.minimum(me + k, slices - 1)))
    return [
        (when, pltpu.make_async_copy(source, x_ref.at[at], sems.at[i]))
        for i, (when, source, at) in enumerate(todo)
    ]


def run(when, action):
    if when is None:
        action()
    else:
        pl.when(when)(action)


def gradient_kernel(kept, dp, slices, meta_s, up_h, own_h, *refs):
    came, (keep_ref, send_ref, x_ref, up_ref, store, sems) = refs[:-6], refs[-6:]
    side = keep_ref.shape[1]
    per = x_ref.shape[2] // side
    blocks = dp * kept
    me = lax.axis_index("dp")
    up_copy = pltpu.make_async_copy(up_h, up_ref, sems.at[len(came) + 1])
    copies = token_copies(slices, own_h, came, x_ref, sems)
    up_copy.start()
    for when, copy in copies:
        run(when, copy.start)
    store[0:blocks] = jnp.zeros((blocks, side, side), f32)
    up_copy.wait()
    for when, copy in copies:
        run(when, copy.wait)
    for b in range(blocks):
        row, col, dest = meta_s[b, 0], meta_s[b, 1], meta_s[b, 2]
        x = x_ref[row // per, :, pl.ds(pl.multiple_of((row % per) * side, side), side)]
        grad = lax.dot_general(
            x, lanes(up_ref, col, side), (((0,), (0,)), ((), ())), preferred_element_type=f32
        )
        gap = jnp.bitwise_xor(jnp.maximum(dest, 0) // kept, me)
        place = (gap & 1) * (dp // 2) + lax.shift_right_logical(gap, 1)
        slot = jnp.where(dest >= 0, place * kept + jnp.maximum(dest, 0) % kept, blocks)
        store[slot] = grad * grad_scale
    half = keep_ref.shape[0]
    keep_ref[...] = store[0:half]
    send_ref[...] = store[half : 2 * half].astype(bf16)


def gradient(meta, own, came, upstream, kept, dp, slices):
    side = meta.shape[1]
    blocks = dp * kept
    half = blocks // 2
    return pl.pallas_call(
        functools.partial(gradient_kernel, kept, dp, slices),
        out_shape=(
            jax.ShapeDtypeStruct((half, side, side), f32),
            jax.ShapeDtypeStruct((half, side, side), bf16),
        ),
        in_specs=[SMEM] + [ANY] * (2 + len(came)),
        out_specs=(VMEM, VMEM),
        scratch_shapes=[
            pltpu.VMEM((slices, *own.shape), bf16),
            pltpu.VMEM(upstream.shape, bf16),
            pltpu.VMEM((blocks + 1, side, side), f32),
            pltpu.SemaphoreType.DMA((len(came) + 2,)),
        ],
        compiler_params=params(),
        cost_estimate=pl.CostEstimate(flops=0, bytes_accessed=0, transcendentals=0),
        name="weight_gradient",
    )(meta, upstream, own, *came)


def slot_reduce(keep, send, kept, dp):
    came = lax.ppermute(send, "dp", [(i, i ^ 1) for i in range(dp)])
    total = keep + came.astype(f32)
    totals = [total[:kept]]
    for gap in range(1, dp // 2):
        totals.append(total[gap * kept : (gap + 1) * kept].astype(bf16))
    parts = totals[:1]
    for gap in range(1, dp // 2):
        parts.append(lax.ppermute(totals[gap], "dp", [(i, i ^ (2 * gap)) for i in range(dp)]))
    return parts, totals


def forward_kernel(kept, ids, slices, meta_s, *refs):
    count = len(ids)
    packs, own_h, came = refs[:count], refs[count], refs[count + 1 : -4]
    out_ref, x_ref, acc, sems = refs[-4:]
    side = packs[0].shape[1]
    pitch = side + TILE
    per = x_ref.shape[2] // side
    copies = token_copies(slices, own_h, came, x_ref, sems)
    for when, copy in copies:
        run(when, copy.start)
    acc[...] = jnp.zeros_like(acc)
    for when, copy in copies:
        run(when, copy.wait)
    for at, ident in enumerate(ids):
        for s in range(kept):
            row = meta_s[ident * kept + s, 0]
            col = meta_s[ident * kept + s, 1]
            x = x_ref[row // per, :, pl.ds(pl.multiple_of((row % per) * side, side), side)]
            part = jnp.dot(
                x, packs[at][s * pitch : s * pitch + side, :], preferred_element_type=f32
            )
            place = pl.ds(pl.multiple_of(col * side, side), side)
            acc[:, place] = acc[:, place] + part
    out_ref[...] = (acc[...] * grad_scale).astype(bf16)


def forward(meta, packs, ids, own, came, kept, slices, hidden):
    tokens = own.shape[0]
    side = meta.shape[1]
    return pl.pallas_call(
        functools.partial(forward_kernel, kept, ids, slices),
        out_shape=jax.ShapeDtypeStruct((tokens, hidden), bf16),
        in_specs=[SMEM] + [VMEM] * len(ids) + [ANY] * (1 + len(came)),
        out_specs=VMEM,
        scratch_shapes=[
            pltpu.VMEM((slices, *own.shape), bf16),
            pltpu.VMEM((tokens, hidden), f32),
            pltpu.SemaphoreType.DMA((len(came) + 1,)),
        ],
        compiler_params=params(),
        cost_estimate=pl.CostEstimate(flops=0, bytes_accessed=0, transcendentals=0),
        name="hidden_out",
    )(meta, *packs, own, *came)


def update_kernel(
    dp, meta_s, w_ref, one_ref, two_ref, left_ref, right_ref, *refs
):
    parts, (new_w, new_one, new_two) = refs[:-3], refs[-3:]
    kept, side = w_ref.shape[0], w_ref.shape[1]
    travel = 3 * side
    me = lax.axis_index("dp")
    source = [jnp.int32(-1)] * kept

    def place(source, dest, here, code):
        mine = here & (dest >= 0) & (jnp.maximum(dest, 0) // kept == me)
        slot = jnp.maximum(dest, 0) % kept
        found = [jnp.where(mine & (slot == q), code, source[q]) for q in range(kept)]
        return found, code + mine.astype(jnp.int32)

    for s in range(kept):
        source, _ = place(source, meta_s[s, 2], True, jnp.int32(s))
    for side_at, other in ((kept, me - 1), (kept + kept // 2, me + 1)):
        here = (other >= 0) & (other < dp)
        gap = jnp.where(here, jnp.bitwise_xor(jnp.clip(other, 0, dp - 1), me), 0)
        code = jnp.int32(side_at)
        for s in range(kept):
            source, code = place(source, meta_s[gap * kept + s, 2], here, code)

    for q in range(kept):

        def write(weight, one, two, q=q):
            grad = parts[0][q]
            for part in parts[1:]:
                grad = grad + part[q].astype(f32)
            first = beta_first * one + (1.0 - beta_first) * grad
            second = beta_second * two + (1.0 - beta_second) * grad * grad
            stepped = weight - learn_rate * first / (jnp.sqrt(second) + epsilon)
            new_w[q] = stepped.astype(bf16)
            new_one[q] = first
            new_two[q] = second

        @pl.when(source[q] < 0)
        def _(q=q):
            new_w[q] = jnp.zeros((side, side), bf16)
            new_one[q] = jnp.zeros((side, side), f32)
            new_two[q] = jnp.zeros((side, side), f32)

        @pl.when((source[q] >= 0) & (source[q] < kept))
        def _(q=q):
            s = jnp.clip(source[q], 0, kept - 1)
            write(w_ref[s].astype(f32), one_ref[s], two_ref[s])

        for ref, first_code in ((left_ref, kept), (right_ref, kept + kept // 2)):

            @pl.when((source[q] >= first_code) & (source[q] < first_code + kept // 2))
            def _(q=q, ref=ref, first_code=first_code):
                rank = jnp.clip(source[q] - first_code, 0, kept // 2 - 1)
                base = pl.multiple_of(rank * travel, TILE)
                write(
                    ref[pl.ds(base, side), :].astype(f32),
                    ref[pl.ds(base + side, side), :].astype(f32),
                    ref[pl.ds(base + 2 * side, side), :].astype(f32),
                )


def update(meta, parts, weight, one, two, from_left, from_right, dp):
    shape = weight.shape
    return pl.pallas_call(
        functools.partial(update_kernel, dp),
        out_shape=(
            jax.ShapeDtypeStruct(shape, bf16),
            jax.ShapeDtypeStruct(shape, f32),
            jax.ShapeDtypeStruct(shape, f32),
        ),
        in_specs=[SMEM] + [VMEM] * (5 + len(parts)),
        out_specs=(VMEM,) * 3,
        compiler_params=params(),
        cost_estimate=pl.CostEstimate(flops=0, bytes_accessed=0, transcendentals=0),
        name="adam_update",
    )(meta, weight, one, two, from_left, from_right, *parts)


def body(weight, moment_one, moment_two, block_row, block_col, dest_slot, tokens, upstream):
    kept = weight.shape[0]
    dp = lax.axis_size("dp")
    slices = lax.axis_size("mp")
    four = slices == 4
    pairs, inner = [(0, 1), (1, 0), (2, 3), (3, 2)], [(1, 2), (2, 1)]
    inward, outward = [(0, 1), (3, 2)], [(1, 0), (2, 3)]

    packs, ids = [pack(block_row, block_col, dest_slot, weight)], [0]
    if four:
        own_tokens = after(tokens, packs[0])
        near = lax.ppermute(own_tokens, "mp", pairs)
        middle = lax.ppermute(own_tokens, "mp", inner)
    else:
        came = line_gather(tokens, "mp")
    bit = dp // 2
    while bit:
        packs = packs + [
            lax.ppermute(p, "dp", [(i, i ^ bit) for i in range(dp)]) for p in packs
        ]
        ids = ids + [i ^ bit for i in ids]
        bit //= 2
        if bit == 1:
            held = hold(after(upstream, packs[1]), packs[0])
            packs[-1] = after(packs[-1], *held)
            packs[0], up_held = held[1], held[0]
    ids = tuple(ids)
    middles = ()
    if four:
        near, middle, packs[-1] = lax.optimization_barrier((near, middle, packs[-1]))
        middles = (middle,)
    shares, meta, mixed = backward(
        packs, ids, up_held, middles, kept, slices, tokens.shape[1]
    )

    dest_leave = dest_slot
    if four:
        outer = lax.rem(lax.axis_index("mp"), 3) == 0
        own_share, far, second, first = shares
        mixed = lax.ppermute(mixed[0], "mp", inward + outward)
        near_on = lax.ppermute(after(near, meta), "mp", inner)
        dest_leave = after(dest_slot, meta)
    to_left, to_right = leave(dest_leave, weight, moment_one, moment_two)
    from_left = lax.ppermute(to_right, "dp", [(i, i + 1) for i in range(dp - 1)])
    from_right = lax.ppermute(to_left, "dp", [(i + 1, i) for i in range(dp - 1)])
    meta_grad = meta
    if four:
        far, mixed, from_left, from_right = lax.optimization_barrier(
            (far, mixed, from_left, from_right)
        )
        sum_far = inner_sum(far, mixed)
        mixed_on = choose(after(second, sum_far), near_on)
        sum_far, mixed_on = lax.optimization_barrier((sum_far, mixed_on))
        mixed_on = lax.ppermute(mixed_on, "mp", inward + outward)
        passed_far = lax.ppermute(sum_far, "mp", inner)
        came = (near, middle, near_on, mixed, mixed_on)
    keep, send = gradient(meta_grad, tokens, came, upstream, kept, dp, slices)
    parts, totals = slot_reduce(keep, send, kept, dp)
    meta_out = meta
    if four:
        sum_second = plus(after(second, send), mixed_on)
        sum_first = plus(after(first, send), passed_far)
        sum_second, sum_first = lax.optimization_barrier((sum_second, sum_first))
        passed_second = lax.ppermute(sum_second, "mp", inner)
        came_first = lax.ppermute(sum_first, "mp", inward + outward)
        meta_out = after(meta, sum_second, sum_first, *totals)
    hidden_out = forward(
        meta_out, packs, ids, tokens, came, kept, slices, upstream.shape[1]
    )
    new_weight, new_first, new_second = update(
        meta, parts, weight, moment_one, moment_two, from_left, from_right, dp
    )
    if four:
        input_grad = (
            after(own_share, hidden_out, new_weight) + came_first.astype(f32) + passed_second.astype(f32)
        ).astype(bf16)
    else:
        input_grad = line_reduce(shares, "mp")
    return (new_weight, new_first, new_second, hidden_out, input_grad)


def solution(mesh):
    blocks = P(("dp", "mp"), None, None)
    ints = P(("dp", "mp"))
    acts = P("dp", "mp")
    return jax.shard_map(
        body,
        mesh=mesh,
        in_specs=(blocks, blocks, blocks, ints, ints, ints, acts, acts),
        out_specs=(blocks, blocks, blocks, acts, acts),
        check_vma=False,
    )
```

```python
import functools
import math

import jax
import jax.numpy as jnp
from jax import lax
from jax.experimental import pallas as pl
from jax.experimental.pallas import tpu as pltpu
from jax.sharding import PartitionSpec as P

D = 8192
TILE = 16

learn_rate = 0.02
beta_first = 0.9
beta_second = 0.95
epsilon = 1e-08
grad_scale = 1.0 / math.sqrt(D)

f32 = jnp.float32
bf16 = jnp.bfloat16
VMEM = pl.BlockSpec(memory_space=pltpu.VMEM)
ANY = pl.BlockSpec(memory_space=pl.ANY)
SMEM = pl.BlockSpec(memory_space=pltpu.SMEM)
HBM = pl.BlockSpec(memory_space=pltpu.HBM)


def params(mib=24):
    return pltpu.CompilerParams(vmem_limit_bytes=mib * 1024 * 1024)


def lanes(ref, index, width):
    return ref[:, pl.ds(pl.multiple_of(index * width, width), width)]


def pack_kernel(row_h, col_h, dest_h, w_h, pack_ref, row_s, col_s, dest_s, w_ref, sems):
    kept, side = w_ref.shape[0], w_ref.shape[1]
    pitch = side + TILE
    copies = [
        pltpu.make_async_copy(source, target, sems.at[i])
        for i, (source, target) in enumerate(
            ((row_h, row_s), (col_h, col_s), (dest_h, dest_s), (w_h, w_ref))
        )
    ]
    for copy in copies:
        copy.start()
    for copy in copies:
        copy.wait()
    lane = lax.broadcasted_iota(jnp.int32, (TILE, side), 1)
    for s in range(kept):
        tile = jnp.where(lane == 0, row_s[s], jnp.where(lane == 1, col_s[s], dest_s[s]))
        pack_ref[s * pitch : s * pitch + side, :] = w_ref[s]
        pack_ref[s * pitch + side : (s + 1) * pitch, :] = tile.astype(f32).astype(bf16)


def pack(rows, cols, dests, weight):
    kept, side, _ = weight.shape
    return pl.pallas_call(
        pack_kernel,
        out_shape=jax.ShapeDtypeStruct((kept * (side + TILE), side), bf16),
        in_specs=[ANY] * 4,
        out_specs=VMEM,
        scratch_shapes=[pltpu.SMEM((kept,), jnp.int32)] * 3
        + [pltpu.VMEM(weight.shape, bf16), pltpu.SemaphoreType.DMA((4,))],
        compiler_params=params(60),
        cost_estimate=pl.CostEstimate(flops=0, bytes_accessed=0, transcendentals=0),
        name="pack_blocks",
    )(rows, cols, dests, weight)


def hold_kernel(count, *refs):
    sems = refs[-1]
    copies = [
        pltpu.make_async_copy(refs[i], refs[count + i], sems.at[i]) for i in range(count)
    ]
    for copy in copies:
        copy.start()
    for copy in copies:
        copy.wait()


def hold(*arrays):
    count = len(arrays)
    return pl.pallas_call(
        functools.partial(hold_kernel, count),
        out_shape=tuple(jax.ShapeDtypeStruct(a.shape, a.dtype) for a in arrays),
        in_specs=[ANY] * count,
        out_specs=(VMEM,) * count,
        scratch_shapes=[pltpu.SemaphoreType.DMA((count,))],
        compiler_params=params(8),
        cost_estimate=pl.CostEstimate(flops=0, bytes_accessed=0, transcendentals=0),
        name="hold_arrays",
    )(*arrays)


def leave_kernel(dest_h, w_h, one_h, two_h, left_ref, right_ref, dest_s, w_ref, one_ref, two_ref, sems):
    kept, side = w_ref.shape[0], w_ref.shape[1]
    half = kept // 2
    me = lax.axis_index("dp")
    travel = 3 * side
    copies = [
        pltpu.make_async_copy(source, target, sems.at[i])
        for i, (source, target) in enumerate(
            ((dest_h, dest_s), (w_h, w_ref), (one_h, one_ref), (two_h, two_ref))
        )
    ]
    for copy in copies:
        copy.start()
    left_ref[...] = jnp.zeros_like(left_ref)
    right_ref[...] = jnp.zeros_like(right_ref)
    for copy in copies:
        copy.wait()
    to_left = jnp.int32(0)
    to_right = jnp.int32(0)
    for s in range(kept):
        dest = dest_s[s]
        goal = jnp.where(dest >= 0, dest // kept, me)
        for ref, count, going in (
            (left_ref, to_left, goal < me),
            (right_ref, to_right, goal > me),
        ):

            @pl.when(going)
            def _(ref=ref, count=count, s=s):
                base = pl.multiple_of(jnp.minimum(count, half - 1) * travel, TILE)
                ref[pl.ds(base, side), :] = w_ref[s]
                ref[pl.ds(base + side, side), :] = one_ref[s].astype(bf16)
                ref[pl.ds(base + 2 * side, side), :] = two_ref[s].astype(bf16)

        to_left = to_left + (goal < me).astype(jnp.int32)
        to_right = to_right + (goal > me).astype(jnp.int32)


def leave(dests, weight, one, two):
    kept, side, _ = weight.shape
    travel = jax.ShapeDtypeStruct((kept // 2 * 3 * side, side), bf16)
    return pl.pallas_call(
        leave_kernel,
        out_shape=(travel, travel),
        in_specs=[ANY] * 4,
        out_specs=(VMEM, VMEM),
        scratch_shapes=[
            pltpu.SMEM((kept,), jnp.int32),
            pltpu.VMEM(weight.shape, bf16),
            pltpu.VMEM(weight.shape, f32),
            pltpu.VMEM(weight.shape, f32),
            pltpu.SemaphoreType.DMA((4,)),
        ],
        compiler_params=params(8),
        cost_estimate=pl.CostEstimate(flops=0, bytes_accessed=0, transcendentals=0),
        name="leaving_blocks",
    )(dests, weight, one, two)


def line_gather(own, axis):
    n = lax.axis_size(axis)
    below, above = [own], [own]
    for step in range(1, n):
        below.append(lax.ppermute(below[-1], axis, [(i, i + 1) for i in range(step - 1, n - 1)]))
        above.append(lax.ppermute(above[-1], axis, [(i + 1, i) for i in range(n - step)]))
    return (*below[1:], *above[1:])


def backward_kernel(kept, ids, slices, *refs):
    count = len(ids)
    packs, up_ref = refs[:count], refs[count]
    acc, meta_s, *held, sems = refs[-3 - slices :]
    refs = refs[count + 1 : -3 - slices]
    shares, meta_ref = refs[:slices], refs[slices]
    side = meta_ref.shape[1]
    pitch = side + TILE
    width = shares[0].shape[1]
    for at, ident in enumerate(ids):
        for s in range(kept):
            tile = packs[at][s * pitch + side : (s + 1) * pitch, :].astype(f32)
            row = ident * kept + s
            meta_ref[row : row + 1, :] = tile[0:1, :].astype(jnp.int32)
    copy = pltpu.make_async_copy(meta_ref, meta_s, sems.at[slices])
    copy.start()
    acc[...] = jnp.zeros_like(acc)
    copy.wait()
    for at, ident in enumerate(ids):
        for s in range(kept):
            row = meta_s[ident * kept + s, 0]
            col = meta_s[ident * kept + s, 1]
            part = lax.dot_general(
                lanes(up_ref, col, side),
                packs[at][s * pitch : s * pitch + side, :],
                (((1,), (1,)), ((), ())),
                preferred_element_type=f32,
            )
            place = pl.ds(pl.multiple_of(row * side, side), side)
            acc[:, place] = acc[:, place] + part
    order = share_order(lax.axis_index("mp"), slices)
    copies = [pltpu.make_async_copy(held[k], shares[k], sems.at[k]) for k in range(slices)]
    for k, quarter in enumerate(order):
        share = lanes(acc, quarter, width) * grad_scale
        held[k][...] = share.astype(held[k].dtype)
        copies[k].start()
    for copy in copies:
        copy.wait()


def share_order(me, slices):
    if slices == 4:
        low = me < 2
        return (me, jnp.where(low, 3, 0), jnp.where(low, 2, 1), jnp.bitwise_xor(me, 1))
    return tuple(lax.rem(me + k, slices) for k in range(slices))


def backward(packs, ids, upstream, kept, slices, features):
    tokens = upstream.shape[0]
    side = packs[0].shape[1]
    blocks = len(ids) * kept
    shares = [
        jax.ShapeDtypeStruct((tokens, features), f32 if k == 0 else bf16) for k in range(slices)
    ]
    outs = pl.pallas_call(
        functools.partial(backward_kernel, kept, ids, slices),
        out_shape=(*shares, jax.ShapeDtypeStruct((blocks, side), jnp.int32)),
        in_specs=[VMEM] * (len(ids) + 1),
        out_specs=(HBM,) * slices + (VMEM,),
        scratch_shapes=[
            pltpu.VMEM((tokens, slices * features), f32),
            pltpu.SMEM((blocks, side), jnp.int32),
            *(pltpu.VMEM(share.shape, share.dtype) for share in shares),
            pltpu.SemaphoreType.DMA((slices + 1,)),
        ],
        compiler_params=params(),
        cost_estimate=pl.CostEstimate(flops=0, bytes_accessed=0, transcendentals=0),
        name="input_gradient",
    )(*packs, upstream)
    return outs[:slices], outs[slices]


def line_reduce(shares, axis):
    n = len(shares)
    right = left = None
    for step in range(1, n):
        to_right, to_left = shares[n - step], shares[step]
        if right is not None:
            to_right = (to_right.astype(f32) + right.astype(f32)).astype(bf16)
            to_left = (to_left.astype(f32) + left.astype(f32)).astype(bf16)
        right = lax.ppermute(to_right, axis, [(i, i + 1) for i in range(step)])
        left = lax.ppermute(to_left, axis, [(n - 1 - i, n - 2 - i) for i in range(step)])
    if right is None:
        return shares[0].astype(bf16)
    return (shares[0] + right.astype(f32) + left.astype(f32)).astype(bf16)


def after(value, *others):
    return lax.optimization_barrier((value, *others))[0]


def sum_kernel(far_h, came_h, sum_ref, far_ref, came_ref, sems):
    @pl.when(lax.rem(lax.axis_index("mp"), 3) != 0)
    def _():
        copies = [
            pltpu.make_async_copy(far_h, far_ref, sems.at[0]),
            pltpu.make_async_copy(came_h, came_ref, sems.at[1]),
        ]
        for copy in copies:
            copy.start()
        for copy in copies:
            copy.wait()
        sum_ref[...] = (far_ref[...].astype(f32) + came_ref[...].astype(f32)).astype(bf16)


def inner_sum(far, came):
    return pl.pallas_call(
        sum_kernel,
        out_shape=jax.ShapeDtypeStruct(far.shape, bf16),
        in_specs=[ANY] * 2,
        out_specs=VMEM,
        scratch_shapes=[
            pltpu.VMEM(far.shape, bf16),
            pltpu.VMEM(far.shape, bf16),
            pltpu.SemaphoreType.DMA((2,)),
        ],
        compiler_params=params(),
        cost_estimate=pl.CostEstimate(flops=0, bytes_accessed=0, transcendentals=0),
        name="inner_sum",
    )(far, came)


def choose_kernel(outer_h, inner_h, mixed_ref, sem):
    outer = lax.rem(lax.axis_index("mp"), 3) == 0
    for when, source in ((outer, outer_h), (jnp.logical_not(outer), inner_h)):

        @pl.when(when)
        def _(source=source):
            copy = pltpu.make_async_copy(source, mixed_ref, sem)
            copy.start()
            copy.wait()


def choose(at_outer, at_inner):
    return pl.pallas_call(
        choose_kernel,
        out_shape=jax.ShapeDtypeStruct(at_outer.shape, bf16),
        in_specs=[ANY] * 2,
        out_specs=VMEM,
        scratch_shapes=[pltpu.SemaphoreType.DMA],
        compiler_params=params(),
        cost_estimate=pl.CostEstimate(flops=0, bytes_accessed=0, transcendentals=0),
        name="choose_sent",
    )(at_outer, at_inner)


def plus(share, came):
    return (share.astype(f32) + came.astype(f32)).astype(bf16)


def token_copies(slices, own, came, x_ref, sems):
    me = lax.axis_index("mp")
    todo = [(None, own, me)]
    if slices == 4:
        near, middle, near_on, mixed = came
        outer = lax.rem(me, 3) == 0
        todo.append((None, near, jnp.bitwise_xor(me, 1)))
        todo.append((outer, mixed, jnp.where(me == 0, 2, 1)))
        todo.append((jnp.logical_not(outer), middle, 3 - me))
        todo.append((jnp.logical_not(outer), near_on, jnp.where(me == 1, 3, 0)))
    else:
        for k in range(1, slices):
            todo.append((me >= k, came[k - 1], jnp.maximum(me - k, 0)))
            todo.append((me + k < slices, came[slices + k - 2], jnp.minimum(me + k, slices - 1)))
    return [
        (when, pltpu.make_async_copy(source, x_ref.at[at], sems.at[i]))
        for i, (when, source, at) in enumerate(todo)
    ]


def run(when, action):
    if when is None:
        action()
    else:
        pl.when(when)(action)


def assemble_kernel(slices, own_h, *refs):
    came, (x_ref, sems) = refs[:-2], refs[-2:]
    copies = token_copies(slices, own_h, came, x_ref, sems)
    for when, copy in copies:
        run(when, copy.start)
    for when, copy in copies:
        run(when, copy.wait)


def assemble(own, came, slices):
    return pl.pallas_call(
        functools.partial(assemble_kernel, slices),
        out_shape=jax.ShapeDtypeStruct((slices, *own.shape), bf16),
        in_specs=[ANY] * (1 + len(came)),
        out_specs=VMEM,
        scratch_shapes=[pltpu.SemaphoreType.DMA((len(came) + 1,))],
        compiler_params=params(),
        cost_estimate=pl.CostEstimate(flops=0, bytes_accessed=0, transcendentals=0),
        name="assemble_tokens",
    )(own, *came)


def token_block(x_ref, last, row, side):
    per = x_ref.shape[2] // side
    place = pl.ds(pl.multiple_of((row % per) * side, side), side)
    block = x_ref[row // per, :, place]
    if last:
        me = lax.axis_index("mp")
        far_end = (lax.rem(me, 3) == 0) & (row // per == 3 - me)
        block = jnp.where(far_end, last[0][:, place], block)
    return block


def gradient_kernel(kept, dp, meta_s, up_ref, x_ref, *refs):
    last, (keep_ref, send_ref, store) = refs[:-3], refs[-3:]
    side = keep_ref.shape[2]
    blocks = dp * kept
    me = lax.axis_index("dp")
    store[0:blocks] = jnp.zeros((blocks, side, side), f32)
    for b in range(blocks):
        row, col, dest = meta_s[b, 0], meta_s[b, 1], meta_s[b, 2]
        grad = lax.dot_general(
            token_block(x_ref, last, row, side),
            lanes(up_ref, col, side),
            (((0,), (0,)), ((), ())),
            preferred_element_type=f32,
        )
        gap = jnp.bitwise_xor(jnp.maximum(dest, 0) // kept, me)
        place = (gap & 1) * (dp // 2) + lax.shift_right_logical(gap, 1)
        slot = jnp.where(dest >= 0, place * kept + jnp.maximum(dest, 0) % kept, blocks)
        store[slot] = grad * grad_scale
    half = keep_ref.shape[0]
    keep_ref[...] = store[0:half]
    send_ref[...] = store[half : 2 * half].astype(bf16)


def gradient(meta, x_all, last, upstream, kept, dp):
    side = meta.shape[1]
    blocks = dp * kept
    half = blocks // 2
    return pl.pallas_call(
        functools.partial(gradient_kernel, kept, dp),
        out_shape=(
            jax.ShapeDtypeStruct((half, side, side), f32),
            jax.ShapeDtypeStruct((half, side, side), bf16),
        ),
        in_specs=[SMEM] + [VMEM] * (2 + len(last)),
        out_specs=(VMEM, VMEM),
        scratch_shapes=[pltpu.VMEM((blocks + 1, side, side), f32)],
        compiler_params=params(),
        cost_estimate=pl.CostEstimate(flops=0, bytes_accessed=0, transcendentals=0),
        name="weight_gradient",
    )(meta, upstream, x_all, *last)


def slot_reduce(keep, send, kept, dp):
    came = lax.ppermute(send, "dp", [(i, i ^ 1) for i in range(dp)])
    total = keep + came.astype(f32)
    totals = [total[:kept]]
    for gap in range(1, dp // 2):
        totals.append(total[gap * kept : (gap + 1) * kept].astype(bf16))
    parts = totals[:1]
    for gap in range(1, dp // 2):
        parts.append(lax.ppermute(totals[gap], "dp", [(i, i ^ (2 * gap)) for i in range(dp)]))
    return parts, totals


def forward_kernel(kept, ids, meta_s, *refs):
    count = len(ids)
    packs, x_ref, last, (out_ref, acc) = refs[:count], refs[count], refs[count + 1 : -2], refs[-2:]
    side = packs[0].shape[1]
    pitch = side + TILE
    acc[...] = jnp.zeros_like(acc)
    for at, ident in enumerate(ids):
        for s in range(kept):
            row = meta_s[ident * kept + s, 0]
            col = meta_s[ident * kept + s, 1]
            part = jnp.dot(
                token_block(x_ref, last, row, side),
                packs[at][s * pitch : s * pitch + side, :],
                preferred_element_type=f32,
            )
            place = pl.ds(pl.multiple_of(col * side, side), side)
            acc[:, place] = acc[:, place] + part
    out_ref[...] = (acc[...] * grad_scale).astype(bf16)


def forward(meta, packs, ids, x_all, last, kept, hidden):
    tokens = x_all.shape[1]
    return pl.pallas_call(
        functools.partial(forward_kernel, kept, ids),
        out_shape=jax.ShapeDtypeStruct((tokens, hidden), bf16),
        in_specs=[SMEM] + [VMEM] * (len(ids) + 1 + len(last)),
        out_specs=VMEM,
        scratch_shapes=[pltpu.VMEM((tokens, hidden), f32)],
        compiler_params=params(),
        cost_estimate=pl.CostEstimate(flops=0, bytes_accessed=0, transcendentals=0),
        name="hidden_out",
    )(meta, *packs, x_all, *last)


def finish_kernel(own_ref, first_ref, second_ref, out_ref):
    total = own_ref[...] + first_ref[...].astype(f32) + second_ref[...].astype(f32)
    out_ref[...] = total.astype(bf16)


def finish(own, first, second):
    return pl.pallas_call(
        finish_kernel,
        out_shape=jax.ShapeDtypeStruct(own.shape, bf16),
        in_specs=[VMEM] * 3,
        out_specs=VMEM,
        compiler_params=params(),
        cost_estimate=pl.CostEstimate(flops=0, bytes_accessed=0, transcendentals=0),
        name="finish_input_grad",
    )(own, first, second)


def update_kernel(
    dp, meta_s, w_ref, one_ref, two_ref, left_ref, right_ref, *refs
):
    parts, (new_w, new_one, new_two) = refs[:-3], refs[-3:]
    kept, side = w_ref.shape[0], w_ref.shape[1]
    travel = 3 * side
    me = lax.axis_index("dp")
    source = [jnp.int32(-1)] * kept

    def place(source, dest, here, code):
        mine = here & (dest >= 0) & (jnp.maximum(dest, 0) // kept == me)
        slot = jnp.maximum(dest, 0) % kept
        found = [jnp.where(mine & (slot == q), code, source[q]) for q in range(kept)]
        return found, code + mine.astype(jnp.int32)

    for s in range(kept):
        source, _ = place(source, meta_s[s, 2], True, jnp.int32(s))
    for side_at, other in ((kept, me - 1), (kept + kept // 2, me + 1)):
        here = (other >= 0) & (other < dp)
        gap = jnp.where(here, jnp.bitwise_xor(jnp.clip(other, 0, dp - 1), me), 0)
        code = jnp.int32(side_at)
        for s in range(kept):
            source, code = place(source, meta_s[gap * kept + s, 2], here, code)

    for q in range(kept):

        def write(weight, one, two, q=q):
            grad = parts[0][q]
            for part in parts[1:]:
                grad = grad + part[q].astype(f32)
            first = beta_first * one + (1.0 - beta_first) * grad
            second = beta_second * two + (1.0 - beta_second) * grad * grad
            stepped = weight - learn_rate * first / (jnp.sqrt(second) + epsilon)
            new_w[q] = stepped.astype(bf16)
            new_one[q] = first
            new_two[q] = second

        @pl.when(source[q] < 0)
        def _(q=q):
            new_w[q] = jnp.zeros((side, side), bf16)
            new_one[q] = jnp.zeros((side, side), f32)
            new_two[q] = jnp.zeros((side, side), f32)

        @pl.when((source[q] >= 0) & (source[q] < kept))
        def _(q=q):
            s = jnp.clip(source[q], 0, kept - 1)
            write(w_ref[s].astype(f32), one_ref[s], two_ref[s])

        for ref, first_code in ((left_ref, kept), (right_ref, kept + kept // 2)):

            @pl.when((source[q] >= first_code) & (source[q] < first_code + kept // 2))
            def _(q=q, ref=ref, first_code=first_code):
                rank = jnp.clip(source[q] - first_code, 0, kept // 2 - 1)
                base = pl.multiple_of(rank * travel, TILE)
                write(
                    ref[pl.ds(base, side), :].astype(f32),
                    ref[pl.ds(base + side, side), :].astype(f32),
                    ref[pl.ds(base + 2 * side, side), :].astype(f32),
                )


def update(meta, parts, weight, one, two, from_left, from_right, dp):
    shape = weight.shape
    return pl.pallas_call(
        functools.partial(update_kernel, dp),
        out_shape=(
            jax.ShapeDtypeStruct(shape, bf16),
            jax.ShapeDtypeStruct(shape, f32),
            jax.ShapeDtypeStruct(shape, f32),
        ),
        in_specs=[SMEM] + [VMEM] * (5 + len(parts)),
        out_specs=(VMEM,) * 3,
        compiler_params=params(),
        cost_estimate=pl.CostEstimate(flops=0, bytes_accessed=0, transcendentals=0),
        name="adam_update",
    )(meta, weight, one, two, from_left, from_right, *parts)


def body(weight, moment_one, moment_two, block_row, block_col, dest_slot, tokens, upstream):
    kept = weight.shape[0]
    dp = lax.axis_size("dp")
    slices = lax.axis_size("mp")
    four = slices == 4
    pairs, inner = [(0, 1), (1, 0), (2, 3), (3, 2)], [(1, 2), (2, 1)]
    inward, outward = [(0, 1), (3, 2)], [(1, 0), (2, 3)]

    packs, ids = [pack(block_row, block_col, dest_slot, weight)], [0]
    if four:
        near = lax.ppermute(tokens, "mp", pairs)
        middle = lax.ppermute(tokens, "mp", inner)
    else:
        came = line_gather(tokens, "mp")
    for gap in range(2, dp, 2):
        packs.append(lax.ppermute(packs[0], "dp", [(i, i ^ gap) for i in range(dp)]))
        ids.append(gap)
    held = hold(after(upstream, packs[0]), packs[0])
    packs[0], up_held = held[1], held[0]
    packs[1:] = lax.optimization_barrier((*packs[1:], *held))[: len(packs) - 1]
    packs += [lax.ppermute(p, "dp", [(i, i ^ 1) for i in range(dp)]) for p in packs]
    ids = tuple(ids + [i ^ 1 for i in ids])
    shares, meta = backward(packs, ids, up_held, kept, slices, tokens.shape[1])

    dest_leave = dest_slot
    if four:
        outer = lax.rem(lax.axis_index("mp"), 3) == 0
        own_share, far, second, first = shares
        near, middle, far = lax.optimization_barrier((near, middle, far))
        mixed = choose(far, middle)
        near, mixed = lax.optimization_barrier((near, mixed))
        mixed = lax.ppermute(mixed, "mp", inward + outward)
        near_on = lax.ppermute(near, "mp", inner)
        dest_leave = after(dest_slot, meta)
    to_left, to_right = leave(dest_leave, weight, moment_one, moment_two)
    from_left = lax.ppermute(to_right, "dp", [(i, i + 1) for i in range(dp - 1)])
    from_right = lax.ppermute(to_left, "dp", [(i + 1, i) for i in range(dp - 1)])
    if four:
        far, mixed, from_left, from_right = lax.optimization_barrier(
            (far, mixed, from_left, from_right)
        )
        sum_far = inner_sum(far, mixed)
        mixed_on = choose(after(second, sum_far), near_on)
        sum_far, mixed_on = lax.optimization_barrier((sum_far, mixed_on))
        mixed_on = lax.ppermute(mixed_on, "mp", inward + outward)
        passed_far = lax.ppermute(sum_far, "mp", inner)
        came = (near, middle, near_on, mixed)
        x_all = assemble(after(tokens, sum_far), came, slices)
        last = (mixed_on,)
    else:
        x_all, last = assemble(tokens, came, slices), ()
    keep, send = gradient(meta, x_all, last, upstream, kept, dp)
    parts, totals = slot_reduce(keep, send, kept, dp)
    meta_out = meta
    if four:
        sum_second = plus(after(second, send), mixed_on)
        sum_first = plus(after(first, send), passed_far)
        sum_second, sum_first = lax.optimization_barrier((sum_second, sum_first))
        passed_second = lax.ppermute(sum_second, "mp", inner)
        came_first = lax.ppermute(sum_first, "mp", inward + outward)
        meta_out = after(meta, sum_second, sum_first, *totals)
    hidden_out = forward(meta_out, packs, ids, x_all, last, kept, upstream.shape[1])
    new_weight, new_first, new_second = update(
        meta, parts, weight, moment_one, moment_two, from_left, from_right, dp
    )
    if four:
        input_grad = finish(
            after(own_share, hidden_out, new_weight), came_first, passed_second
        )
    else:
        input_grad = line_reduce(shares, "mp")
    return (new_weight, new_first, new_second, hidden_out, input_grad)


def solution(mesh):
    blocks = P(("dp", "mp"), None, None)
    ints = P(("dp", "mp"))
    acts = P("dp", "mp")
    return jax.shard_map(
        body,
        mesh=mesh,
        in_specs=(blocks, blocks, blocks, ints, ints, ints, acts, acts),
        out_specs=(blocks, blocks, blocks, acts, acts),
        check_vma=False,
    )
```

```python
import functools
import math

import jax
import jax.numpy as jnp
from jax import lax
from jax.experimental import pallas as pl
from jax.experimental.pallas import tpu as pltpu
from jax.sharding import PartitionSpec as P

D = 8192
TILE = 16

learn_rate = 0.02
beta_first = 0.9
beta_second = 0.95
epsilon = 1e-08
grad_scale = 1.0 / math.sqrt(D)

f32 = jnp.float32
bf16 = jnp.bfloat16
VMEM = pl.BlockSpec(memory_space=pltpu.VMEM)
ANY = pl.BlockSpec(memory_space=pl.ANY)
SMEM = pl.BlockSpec(memory_space=pltpu.SMEM)


def params(mib=24):
    return pltpu.CompilerParams(vmem_limit_bytes=mib * 1024 * 1024)


def lanes(ref, index, width):
    return ref[:, pl.ds(pl.multiple_of(index * width, width), width)]


def pack_kernel(row_h, col_h, dest_h, w_h, pack_ref, row_s, col_s, dest_s, w_ref, sems):
    kept, side = w_ref.shape[0], w_ref.shape[1]
    pitch = side + TILE
    copies = [
        pltpu.make_async_copy(source, target, sems.at[i])
        for i, (source, target) in enumerate(
            ((row_h, row_s), (col_h, col_s), (dest_h, dest_s), (w_h, w_ref))
        )
    ]
    for copy in copies:
        copy.start()
    for copy in copies:
        copy.wait()
    lane = lax.broadcasted_iota(jnp.int32, (TILE, side), 1)
    for s in range(kept):
        tile = jnp.where(lane == 0, row_s[s], jnp.where(lane == 1, col_s[s], dest_s[s]))
        pack_ref[s * pitch : s * pitch + side, :] = w_ref[s]
        pack_ref[s * pitch + side : (s + 1) * pitch, :] = tile.astype(f32).astype(bf16)


def pack(rows, cols, dests, weight):
    kept, side, _ = weight.shape
    return pl.pallas_call(
        pack_kernel,
        out_shape=jax.ShapeDtypeStruct((kept * (side + TILE), side), bf16),
        in_specs=[ANY] * 4,
        out_specs=VMEM,
        scratch_shapes=[pltpu.SMEM((kept,), jnp.int32)] * 3
        + [pltpu.VMEM(weight.shape, bf16), pltpu.SemaphoreType.DMA((4,))],
        compiler_params=params(60),
        cost_estimate=pl.CostEstimate(flops=0, bytes_accessed=0, transcendentals=0),
        name="pack_blocks",
    )(rows, cols, dests, weight)


def hold_kernel(count, *refs):
    sems = refs[-1]
    copies = [
        pltpu.make_async_copy(refs[i], refs[count + i], sems.at[i]) for i in range(count)
    ]
    for copy in copies:
        copy.start()
    for copy in copies:
        copy.wait()


def hold(*arrays):
    count = len(arrays)
    return pl.pallas_call(
        functools.partial(hold_kernel, count),
        out_shape=tuple(jax.ShapeDtypeStruct(a.shape, a.dtype) for a in arrays),
        in_specs=[ANY] * count,
        out_specs=(VMEM,) * count,
        scratch_shapes=[pltpu.SemaphoreType.DMA((count,))],
        compiler_params=params(8),
        cost_estimate=pl.CostEstimate(flops=0, bytes_accessed=0, transcendentals=0),
        name="hold_arrays",
    )(*arrays)


def leave_kernel(dest_h, w_h, one_h, two_h, left_ref, right_ref, dest_s, w_ref, one_ref, two_ref, sems):
    kept, side = w_ref.shape[0], w_ref.shape[1]
    half = kept // 2
    me = lax.axis_index("dp")
    travel = 3 * side
    copies = [
        pltpu.make_async_copy(source, target, sems.at[i])
        for i, (source, target) in enumerate(
            ((dest_h, dest_s), (w_h, w_ref), (one_h, one_ref), (two_h, two_ref))
        )
    ]
    for copy in copies:
        copy.start()
    left_ref[...] = jnp.zeros_like(left_ref)
    right_ref[...] = jnp.zeros_like(right_ref)
    for copy in copies:
        copy.wait()
    to_left = jnp.int32(0)
    to_right = jnp.int32(0)
    for s in range(kept):
        dest = dest_s[s]
        goal = jnp.where(dest >= 0, dest // kept, me)
        for ref, count, going in (
            (left_ref, to_left, goal < me),
            (right_ref, to_right, goal > me),
        ):

            @pl.when(going)
            def _(ref=ref, count=count, s=s):
                base = pl.multiple_of(jnp.minimum(count, half - 1) * travel, TILE)
                ref[pl.ds(base, side), :] = w_ref[s]
                ref[pl.ds(base + side, side), :] = one_ref[s].astype(bf16)
                ref[pl.ds(base + 2 * side, side), :] = two_ref[s].astype(bf16)

        to_left = to_left + (goal < me).astype(jnp.int32)
        to_right = to_right + (goal > me).astype(jnp.int32)


def leave(dests, weight, one, two):
    kept, side, _ = weight.shape
    travel = jax.ShapeDtypeStruct((kept // 2 * 3 * side, side), bf16)
    return pl.pallas_call(
        leave_kernel,
        out_shape=(travel, travel),
        in_specs=[ANY] * 4,
        out_specs=(VMEM, VMEM),
        scratch_shapes=[
            pltpu.SMEM((kept,), jnp.int32),
            pltpu.VMEM(weight.shape, bf16),
            pltpu.VMEM(weight.shape, f32),
            pltpu.VMEM(weight.shape, f32),
            pltpu.SemaphoreType.DMA((4,)),
        ],
        compiler_params=params(8),
        cost_estimate=pl.CostEstimate(flops=0, bytes_accessed=0, transcendentals=0),
        name="leaving_blocks",
    )(dests, weight, one, two)


def line_gather(own, axis):
    n = lax.axis_size(axis)
    below, above = [own], [own]
    for step in range(1, n):
        below.append(lax.ppermute(below[-1], axis, [(i, i + 1) for i in range(step - 1, n - 1)]))
        above.append(lax.ppermute(above[-1], axis, [(i + 1, i) for i in range(n - step)]))
    return (*below[1:], *above[1:])


def backward_kernel(kept, ids, slices, *refs):
    count = len(ids)
    packs, up_ref = refs[:count], refs[count]
    acc, meta_ref, *far_ref = refs[count + 1 : -2]
    meta_s, sem = refs[-2:]
    side = packs[0].shape[1]
    pitch = side + TILE
    width = acc.shape[1] // slices
    for at, ident in enumerate(ids):
        for s in range(kept):
            tile = packs[at][s * pitch + side : (s + 1) * pitch, :].astype(f32)
            row = ident * kept + s
            meta_ref[row : row + 1, :] = tile[0:1, :].astype(jnp.int32)
    copy = pltpu.make_async_copy(meta_ref, meta_s, sem)
    copy.start()
    acc[...] = jnp.zeros_like(acc)
    copy.wait()
    for at, ident in enumerate(ids):
        for s in range(kept):
            row = meta_s[ident * kept + s, 0]
            col = meta_s[ident * kept + s, 1]
            part = lax.dot_general(
                lanes(up_ref, col, side),
                packs[at][s * pitch : s * pitch + side, :],
                (((1,), (1,)), ((), ())),
                preferred_element_type=f32,
            )
            place = pl.ds(pl.multiple_of(row * side, side), side)
            acc[:, place] = acc[:, place] + part
    for ref in far_ref:
        far = share_order(lax.axis_index("mp"), slices)[1]
        ref[...] = (lanes(acc, far, width) * grad_scale).astype(bf16)


def split_kernel(slices, chosen, acc, *shares):
    width = acc.shape[1] // slices
    order = share_order(lax.axis_index("mp"), slices)
    for ref, k in zip(shares, chosen):
        ref[...] = (lanes(acc, order[k], width) * grad_scale).astype(ref.dtype)


def split(acc, slices, chosen):
    shape = (acc.shape[0], acc.shape[1] // slices)
    return pl.pallas_call(
        functools.partial(split_kernel, slices, chosen),
        out_shape=tuple(jax.ShapeDtypeStruct(shape, bf16 if k else f32) for k in chosen),
        in_specs=[VMEM],
        out_specs=(VMEM,) * len(chosen),
        compiler_params=params(),
        cost_estimate=pl.CostEstimate(flops=0, bytes_accessed=0, transcendentals=0),
        name="split_shares",
    )(acc)


def share_order(me, slices):
    if slices == 4:
        low = me < 2
        return (me, jnp.where(low, 3, 0), jnp.where(low, 2, 1), jnp.bitwise_xor(me, 1))
    return tuple(lax.rem(me + k, slices) for k in range(slices))


def backward(packs, ids, upstream, kept, slices, features):
    tokens = upstream.shape[0]
    side = packs[0].shape[1]
    blocks = len(ids) * kept
    far = [jax.ShapeDtypeStruct((tokens, features), bf16)] * (slices == 4)
    return pl.pallas_call(
        functools.partial(backward_kernel, kept, ids, slices),
        out_shape=(
            jax.ShapeDtypeStruct((tokens, slices * features), f32),
            jax.ShapeDtypeStruct((blocks, side), jnp.int32),
            *far,
        ),
        in_specs=[VMEM] * (len(ids) + 1),
        out_specs=(VMEM,) * (2 + len(far)),
        scratch_shapes=[pltpu.SMEM((blocks, side), jnp.int32), pltpu.SemaphoreType.DMA],
        compiler_params=params(),
        cost_estimate=pl.CostEstimate(flops=0, bytes_accessed=0, transcendentals=0),
        name="input_gradient",
    )(*packs, upstream)


def line_reduce(shares, axis):
    n = len(shares)
    right = left = None
    for step in range(1, n):
        to_right, to_left = shares[n - step], shares[step]
        if right is not None:
            to_right = (to_right.astype(f32) + right.astype(f32)).astype(bf16)
            to_left = (to_left.astype(f32) + left.astype(f32)).astype(bf16)
        right = lax.ppermute(to_right, axis, [(i, i + 1) for i in range(step)])
        left = lax.ppermute(to_left, axis, [(n - 1 - i, n - 2 - i) for i in range(step)])
    if right is None:
        return shares[0].astype(bf16)
    return (shares[0] + right.astype(f32) + left.astype(f32)).astype(bf16)


def after(value, *others):
    return lax.optimization_barrier((value, *others))[0]


def sum_kernel(far_h, came_h, sum_ref, far_ref, came_ref, sems):
    @pl.when(lax.rem(lax.axis_index("mp"), 3) != 0)
    def _():
        copies = [
            pltpu.make_async_copy(far_h, far_ref, sems.at[0]),
            pltpu.make_async_copy(came_h, came_ref, sems.at[1]),
        ]
        for copy in copies:
            copy.start()
        for copy in copies:
            copy.wait()
        sum_ref[...] = (far_ref[...].astype(f32) + came_ref[...].astype(f32)).astype(bf16)


def inner_sum(far, came):
    return pl.pallas_call(
        sum_kernel,
        out_shape=jax.ShapeDtypeStruct(far.shape, bf16),
        in_specs=[ANY] * 2,
        out_specs=VMEM,
        scratch_shapes=[
            pltpu.VMEM(far.shape, bf16),
            pltpu.VMEM(far.shape, bf16),
            pltpu.SemaphoreType.DMA((2,)),
        ],
        compiler_params=params(),
        cost_estimate=pl.CostEstimate(flops=0, bytes_accessed=0, transcendentals=0),
        name="inner_sum",
    )(far, came)


def choose_kernel(outer_h, inner_h, mixed_ref, sem):
    outer = lax.rem(lax.axis_index("mp"), 3) == 0
    for when, source in ((outer, outer_h), (jnp.logical_not(outer), inner_h)):

        @pl.when(when)
        def _(source=source):
            copy = pltpu.make_async_copy(source, mixed_ref, sem)
            copy.start()
            copy.wait()


def choose(at_outer, at_inner):
    return pl.pallas_call(
        choose_kernel,
        out_shape=jax.ShapeDtypeStruct(at_outer.shape, bf16),
        in_specs=[ANY] * 2,
        out_specs=VMEM,
        scratch_shapes=[pltpu.SemaphoreType.DMA],
        compiler_params=params(),
        cost_estimate=pl.CostEstimate(flops=0, bytes_accessed=0, transcendentals=0),
        name="choose_sent",
    )(at_outer, at_inner)


def plus(share, came):
    return (share.astype(f32) + came.astype(f32)).astype(bf16)


def token_copies(slices, own, came, x_ref, sems):
    me = lax.axis_index("mp")
    todo = [(None, own, me)]
    if slices == 4:
        near, middle, near_on, mixed = came
        outer = lax.rem(me, 3) == 0
        todo.append((None, near, jnp.bitwise_xor(me, 1)))
        todo.append((outer, mixed, jnp.where(me == 0, 2, 1)))
        todo.append((jnp.logical_not(outer), middle, 3 - me))
        todo.append((jnp.logical_not(outer), near_on, jnp.where(me == 1, 3, 0)))
    else:
        for k in range(1, slices):
            todo.append((me >= k, came[k - 1], jnp.maximum(me - k, 0)))
            todo.append((me + k < slices, came[slices + k - 2], jnp.minimum(me + k, slices - 1)))
    return [
        (when, pltpu.make_async_copy(source, x_ref.at[at], sems.at[i]))
        for i, (when, source, at) in enumerate(todo)
    ]


def run(when, action):
    if when is None:
        action()
    else:
        pl.when(when)(action)


def assemble_kernel(slices, own_h, *refs):
    came, (x_ref, sems) = refs[:-2], refs[-2:]
    copies = token_copies(slices, own_h, came, x_ref, sems)
    for when, copy in copies:
        run(when, copy.start)
    for when, copy in copies:
        run(when, copy.wait)


def assemble(own, came, slices):
    return pl.pallas_call(
        functools.partial(assemble_kernel, slices),
        out_shape=jax.ShapeDtypeStruct((slices, *own.shape), bf16),
        in_specs=[ANY] * (1 + len(came)),
        out_specs=VMEM,
        scratch_shapes=[pltpu.SemaphoreType.DMA((len(came) + 1,))],
        compiler_params=params(),
        cost_estimate=pl.CostEstimate(flops=0, bytes_accessed=0, transcendentals=0),
        name="assemble_tokens",
    )(own, *came)


def token_block(x_ref, last, row, side):
    per = x_ref.shape[2] // side
    place = pl.ds(pl.multiple_of((row % per) * side, side), side)
    block = x_ref[row // per, :, place]
    if last:
        me = lax.axis_index("mp")
        far_end = (lax.rem(me, 3) == 0) & (row // per == 3 - me)
        block = jnp.where(far_end, last[0][:, place], block)
    return block


def turn_kernel(meta_s, up_ref, turned_ref):
    side = turned_ref.shape[1]
    for b in range(turned_ref.shape[0]):
        turned_ref[b] = jnp.transpose(lanes(up_ref, meta_s[b, 1], side))


def turn(meta, upstream):
    blocks, side = meta.shape
    return pl.pallas_call(
        turn_kernel,
        out_shape=jax.ShapeDtypeStruct((blocks, side, upstream.shape[0]), bf16),
        in_specs=[SMEM, VMEM],
        out_specs=VMEM,
        compiler_params=params(),
        cost_estimate=pl.CostEstimate(flops=0, bytes_accessed=0, transcendentals=0),
        name="turn_upstream",
    )(meta, upstream)


def gradient_kernel(kept, dp, meta_s, turned_ref, x_ref, *refs):
    last, (store, send_ref) = refs[:-2], refs[-2:]
    side = store.shape[2]
    blocks = dp * kept
    half = blocks // 2
    me = lax.axis_index("dp")
    for b in range(blocks):
        row, dest = meta_s[b, 0], meta_s[b, 2]
        grad = jnp.dot(
            turned_ref[b], token_block(x_ref, last, row, side), preferred_element_type=f32
        )
        gap = jnp.bitwise_xor(jnp.maximum(dest, 0) // kept, me)
        place = (gap & 1) * (dp // 2) + lax.shift_right_logical(gap, 1)
        slot = jnp.where(dest >= 0, place * kept + jnp.maximum(dest, 0) % kept, blocks)
        store[slot] = grad * grad_scale
    send_ref[...] = store[half : 2 * half].astype(bf16)


def gradient(meta, x_all, last, turned, kept, dp):
    side = meta.shape[1]
    blocks = dp * kept
    half = blocks // 2
    return pl.pallas_call(
        functools.partial(gradient_kernel, kept, dp),
        out_shape=(
            jax.ShapeDtypeStruct((blocks + 1, side, side), f32),
            jax.ShapeDtypeStruct((half, side, side), bf16),
        ),
        in_specs=[SMEM] + [VMEM] * (2 + len(last)),
        out_specs=(VMEM, VMEM),
        compiler_params=params(),
        cost_estimate=pl.CostEstimate(flops=0, bytes_accessed=0, transcendentals=0),
        name="weight_gradient",
    )(meta, turned, x_all, *last)


def slot_reduce(keep, send, kept, dp):
    came = lax.ppermute(send, "dp", [(i, i ^ 1) for i in range(dp)])
    total = keep[: send.shape[0]] + came.astype(f32)
    totals = [total[:kept]]
    for gap in range(1, dp // 2):
        totals.append(total[gap * kept : (gap + 1) * kept].astype(bf16))
    parts = totals[:1]
    for gap in range(1, dp // 2):
        parts.append(lax.ppermute(totals[gap], "dp", [(i, i ^ (2 * gap)) for i in range(dp)]))
    return parts, totals


def forward_kernel(kept, ids, meta_s, *refs):
    count = len(ids)
    packs, x_ref, last, (out_ref, acc) = refs[:count], refs[count], refs[count + 1 : -2], refs[-2:]
    side = packs[0].shape[1]
    pitch = side + TILE
    acc[...] = jnp.zeros_like(acc)
    for at, ident in enumerate(ids):
        for s in range(kept):
            row = meta_s[ident * kept + s, 0]
            col = meta_s[ident * kept + s, 1]
            part = jnp.dot(
                token_block(x_ref, last, row, side),
                packs[at][s * pitch : s * pitch + side, :],
                preferred_element_type=f32,
            )
            place = pl.ds(pl.multiple_of(col * side, side), side)
            acc[:, place] = acc[:, place] + part
    out_ref[...] = (acc[...] * grad_scale).astype(bf16)


def forward(meta, packs, ids, x_all, last, kept, hidden):
    tokens = x_all.shape[1]
    return pl.pallas_call(
        functools.partial(forward_kernel, kept, ids),
        out_shape=jax.ShapeDtypeStruct((tokens, hidden), bf16),
        in_specs=[SMEM] + [VMEM] * (len(ids) + 1 + len(last)),
        out_specs=VMEM,
        scratch_shapes=[pltpu.VMEM((tokens, hidden), f32)],
        compiler_params=params(),
        cost_estimate=pl.CostEstimate(flops=0, bytes_accessed=0, transcendentals=0),
        name="hidden_out",
    )(meta, *packs, x_all, *last)


def finish_kernel(own_ref, first_ref, second_ref, out_ref):
    total = own_ref[...] + first_ref[...].astype(f32) + second_ref[...].astype(f32)
    out_ref[...] = total.astype(bf16)


def finish(own, first, second):
    return pl.pallas_call(
        finish_kernel,
        out_shape=jax.ShapeDtypeStruct(own.shape, bf16),
        in_specs=[VMEM] * 3,
        out_specs=VMEM,
        compiler_params=params(),
        cost_estimate=pl.CostEstimate(flops=0, bytes_accessed=0, transcendentals=0),
        name="finish_input_grad",
    )(own, first, second)


def update_kernel(
    dp, meta_s, w_ref, one_ref, two_ref, left_ref, right_ref, *refs
):
    parts, (new_w, new_one, new_two) = refs[:-3], refs[-3:]
    kept, side = w_ref.shape[0], w_ref.shape[1]
    travel = 3 * side
    me = lax.axis_index("dp")
    source = [jnp.int32(-1)] * kept

    def place(source, dest, here, code):
        mine = here & (dest >= 0) & (jnp.maximum(dest, 0) // kept == me)
        slot = jnp.maximum(dest, 0) % kept
        found = [jnp.where(mine & (slot == q), code, source[q]) for q in range(kept)]
        return found, code + mine.astype(jnp.int32)

    for s in range(kept):
        source, _ = place(source, meta_s[s, 2], True, jnp.int32(s))
    for side_at, other in ((kept, me - 1), (kept + kept // 2, me + 1)):
        here = (other >= 0) & (other < dp)
        gap = jnp.where(here, jnp.bitwise_xor(jnp.clip(other, 0, dp - 1), me), 0)
        code = jnp.int32(side_at)
        for s in range(kept):
            source, code = place(source, meta_s[gap * kept + s, 2], here, code)

    for q in range(kept):

        def write(weight, one, two, q=q):
            grad = parts[0][q]
            for part in parts[1:]:
                grad = grad + part[q].astype(f32)
            grad = jnp.transpose(grad)
            first = beta_first * one + (1.0 - beta_first) * grad
            second = beta_second * two + (1.0 - beta_second) * grad * grad
            stepped = weight - learn_rate * first / (jnp.sqrt(second) + epsilon)
            new_w[q] = stepped.astype(bf16)
            new_one[q] = first
            new_two[q] = second

        @pl.when(source[q] < 0)
        def _(q=q):
            new_w[q] = jnp.zeros((side, side), bf16)
            new_one[q] = jnp.zeros((side, side), f32)
            new_two[q] = jnp.zeros((side, side), f32)

        @pl.when((source[q] >= 0) & (source[q] < kept))
        def _(q=q):
            s = jnp.clip(source[q], 0, kept - 1)
            write(w_ref[s].astype(f32), one_ref[s], two_ref[s])

        for ref, first_code in ((left_ref, kept), (right_ref, kept + kept // 2)):

            @pl.when((source[q] >= first_code) & (source[q] < first_code + kept // 2))
            def _(q=q, ref=ref, first_code=first_code):
                rank = jnp.clip(source[q] - first_code, 0, kept // 2 - 1)
                base = pl.multiple_of(rank * travel, TILE)
                write(
                    ref[pl.ds(base, side), :].astype(f32),
                    ref[pl.ds(base + side, side), :].astype(f32),
                    ref[pl.ds(base + 2 * side, side), :].astype(f32),
                )


def update(meta, parts, weight, one, two, from_left, from_right, dp):
    shape = weight.shape
    return pl.pallas_call(
        functools.partial(update_kernel, dp),
        out_shape=(
            jax.ShapeDtypeStruct(shape, bf16),
            jax.ShapeDtypeStruct(shape, f32),
            jax.ShapeDtypeStruct(shape, f32),
        ),
        in_specs=[SMEM] + [VMEM] * (5 + len(parts)),
        out_specs=(VMEM,) * 3,
        compiler_params=params(),
        cost_estimate=pl.CostEstimate(flops=0, bytes_accessed=0, transcendentals=0),
        name="adam_update",
    )(meta, weight, one, two, from_left, from_right, *parts)


def body(weight, moment_one, moment_two, block_row, block_col, dest_slot, tokens, upstream):
    kept = weight.shape[0]
    dp = lax.axis_size("dp")
    slices = lax.axis_size("mp")
    four = slices == 4
    pairs, inner = [(0, 1), (1, 0), (2, 3), (3, 2)], [(1, 2), (2, 1)]
    inward, outward = [(0, 1), (3, 2)], [(1, 0), (2, 3)]

    packs, ids = [pack(block_row, block_col, dest_slot, weight)], [0]
    if four:
        near = lax.ppermute(tokens, "mp", pairs)
        middle = lax.ppermute(tokens, "mp", inner)
    else:
        came = line_gather(tokens, "mp")
    for gap in range(2, dp, 2):
        packs.append(lax.ppermute(packs[0], "dp", [(i, i ^ gap) for i in range(dp)]))
        ids.append(gap)
    held = hold(after(upstream, packs[0]), packs[0])
    packs[0], up_held = held[1], held[0]
    packs[1:] = lax.optimization_barrier((*packs[1:], *held))[: len(packs) - 1]
    packs += [lax.ppermute(p, "dp", [(i, i ^ 1) for i in range(dp)]) for p in packs]
    ids = tuple(ids + [i ^ 1 for i in ids])
    sums, meta, *far = backward(packs, ids, up_held, kept, slices, tokens.shape[1])

    dest_leave = dest_slot
    if four:
        outer = lax.rem(lax.axis_index("mp"), 3) == 0
        near, middle, far = lax.optimization_barrier((near, middle, far[0]))
        mixed_sent = choose(far, middle)
        near, mixed = lax.optimization_barrier((near, mixed_sent))
        mixed = lax.ppermute(mixed, "mp", inward + outward)
        near_on = lax.ppermute(near, "mp", inner)
        own_share, second, first = split(after(sums, mixed_sent), slices, (0, 2, 3))
        dest_leave = after(dest_slot, own_share)
    to_left, to_right = leave(dest_leave, weight, moment_one, moment_two)
    from_left = lax.ppermute(to_right, "dp", [(i, i + 1) for i in range(dp - 1)])
    from_right = lax.ppermute(to_left, "dp", [(i + 1, i) for i in range(dp - 1)])
    if four:
        far, mixed, from_left, from_right = lax.optimization_barrier(
            (far, mixed, from_left, from_right)
        )
        sum_far = inner_sum(far, mixed)
        mixed_on = choose(after(second, sum_far), near_on)
        sum_far, mixed_on = lax.optimization_barrier((sum_far, mixed_on))
        mixed_on = lax.ppermute(mixed_on, "mp", inward + outward)
        passed_far = lax.ppermute(sum_far, "mp", inner)
        came = (near, middle, near_on, mixed)
        x_all = assemble(after(tokens, sum_far), came, slices)
        turned = turn(after(meta, x_all), upstream)
        last = (mixed_on,)
    else:
        x_all, last = assemble(tokens, came, slices), ()
        turned = turn(meta, upstream)
    keep, send = gradient(meta, x_all, last, turned, kept, dp)
    parts, totals = slot_reduce(keep, send, kept, dp)
    meta_out = meta
    if four:
        sum_second = plus(after(second, send), mixed_on)
        sum_first = plus(after(first, send), passed_far)
        sum_second, sum_first = lax.optimization_barrier((sum_second, sum_first))
        passed_second = lax.ppermute(sum_second, "mp", inner)
        came_first = lax.ppermute(sum_first, "mp", inward + outward)
        meta_out = after(meta, sum_second, sum_first, *totals)
    hidden_out = forward(meta_out, packs, ids, x_all, last, kept, upstream.shape[1])
    new_weight, new_first, new_second = update(
        meta, parts, weight, moment_one, moment_two, from_left, from_right, dp
    )
    if four:
        input_grad = finish(
            after(own_share, hidden_out, new_weight), came_first, passed_second
        )
    else:
        input_grad = line_reduce(split(sums, slices, tuple(range(slices))), "mp")
    return (new_weight, new_first, new_second, hidden_out, input_grad)


def solution(mesh):
    blocks = P(("dp", "mp"), None, None)
    ints = P(("dp", "mp"))
    acts = P("dp", "mp")
    return jax.shard_map(
        body,
        mesh=mesh,
        in_specs=(blocks, blocks, blocks, ints, ints, ints, acts, acts),
        out_specs=(blocks, blocks, blocks, acts, acts),
        check_vma=False,
    )
```

```python
import functools
import math

import jax
import jax.numpy as jnp
from jax import lax
from jax.experimental import pallas as pl
from jax.experimental.pallas import tpu as pltpu
from jax.sharding import PartitionSpec as P

D = 8192
TILE = 16

learn_rate = 0.02
beta_first = 0.9
beta_second = 0.95
epsilon = 1e-08
grad_scale = 1.0 / math.sqrt(D)

f32 = jnp.float32
bf16 = jnp.bfloat16
VMEM = pl.BlockSpec(memory_space=pltpu.VMEM)
ANY = pl.BlockSpec(memory_space=pl.ANY)
SMEM = pl.BlockSpec(memory_space=pltpu.SMEM)


def params(mib=24):
    return pltpu.CompilerParams(vmem_limit_bytes=mib * 1024 * 1024)


def lanes(ref, index, width):
    return ref[:, pl.ds(pl.multiple_of(index * width, width), width)]


def pack_kernel(row_h, col_h, dest_h, w_h, pack_ref, row_s, col_s, dest_s, w_ref, sems):
    kept, side = w_ref.shape[0], w_ref.shape[1]
    pitch = side + TILE
    copies = [
        pltpu.make_async_copy(source, target, sems.at[i])
        for i, (source, target) in enumerate(
            ((row_h, row_s), (col_h, col_s), (dest_h, dest_s), (w_h, w_ref))
        )
    ]
    for copy in copies:
        copy.start()
    for copy in copies:
        copy.wait()
    lane = lax.broadcasted_iota(jnp.int32, (TILE, side), 1)
    for s in range(kept):
        tile = jnp.where(lane == 0, row_s[s], jnp.where(lane == 1, col_s[s], dest_s[s]))
        pack_ref[s * pitch : s * pitch + side, :] = w_ref[s]
        pack_ref[s * pitch + side : (s + 1) * pitch, :] = tile.astype(f32).astype(bf16)


def pack(rows, cols, dests, weight):
    kept, side, _ = weight.shape
    return pl.pallas_call(
        pack_kernel,
        out_shape=jax.ShapeDtypeStruct((kept * (side + TILE), side), bf16),
        in_specs=[ANY] * 4,
        out_specs=VMEM,
        scratch_shapes=[pltpu.SMEM((kept,), jnp.int32)] * 3
        + [pltpu.VMEM(weight.shape, bf16), pltpu.SemaphoreType.DMA((4,))],
        compiler_params=params(60),
        cost_estimate=pl.CostEstimate(flops=0, bytes_accessed=0, transcendentals=0),
        name="pack_blocks",
    )(rows, cols, dests, weight)


def hold_kernel(count, *refs):
    sems = refs[-1]
    copies = [
        pltpu.make_async_copy(refs[i], refs[count + i], sems.at[i]) for i in range(count)
    ]
    for copy in copies:
        copy.start()
    for copy in copies:
        copy.wait()


def hold(*arrays):
    count = len(arrays)
    return pl.pallas_call(
        functools.partial(hold_kernel, count),
        out_shape=tuple(jax.ShapeDtypeStruct(a.shape, a.dtype) for a in arrays),
        in_specs=[ANY] * count,
        out_specs=(VMEM,) * count,
        scratch_shapes=[pltpu.SemaphoreType.DMA((count,))],
        compiler_params=params(8),
        cost_estimate=pl.CostEstimate(flops=0, bytes_accessed=0, transcendentals=0),
        name="hold_arrays",
    )(*arrays)


def leave_kernel(dest_h, w_h, one_h, two_h, left_ref, right_ref, dest_s, w_ref, one_ref, two_ref, sems):
    kept, side = w_ref.shape[0], w_ref.shape[1]
    half = kept // 2
    me = lax.axis_index("dp")
    travel = 3 * side
    copies = [
        pltpu.make_async_copy(source, target, sems.at[i])
        for i, (source, target) in enumerate(
            ((dest_h, dest_s), (w_h, w_ref), (one_h, one_ref), (two_h, two_ref))
        )
    ]
    for copy in copies:
        copy.start()
    left_ref[...] = jnp.zeros_like(left_ref)
    right_ref[...] = jnp.zeros_like(right_ref)
    for copy in copies:
        copy.wait()
    to_left = jnp.int32(0)
    to_right = jnp.int32(0)
    for s in range(kept):
        dest = dest_s[s]
        goal = jnp.where(dest >= 0, dest // kept, me)
        for ref, count, going in (
            (left_ref, to_left, goal < me),
            (right_ref, to_right, goal > me),
        ):

            @pl.when(going)
            def _(ref=ref, count=count, s=s):
                base = pl.multiple_of(jnp.minimum(count, half - 1) * travel, TILE)
                ref[pl.ds(base, side), :] = w_ref[s]
                ref[pl.ds(base + side, side), :] = one_ref[s].astype(bf16)
                ref[pl.ds(base + 2 * side, side), :] = two_ref[s].astype(bf16)

        to_left = to_left + (goal < me).astype(jnp.int32)
        to_right = to_right + (goal > me).astype(jnp.int32)


def leave(dests, weight, one, two):
    kept, side, _ = weight.shape
    travel = jax.ShapeDtypeStruct((kept // 2 * 3 * side, side), bf16)
    return pl.pallas_call(
        leave_kernel,
        out_shape=(travel, travel),
        in_specs=[ANY] * 4,
        out_specs=(VMEM, VMEM),
        scratch_shapes=[
            pltpu.SMEM((kept,), jnp.int32),
            pltpu.VMEM(weight.shape, bf16),
            pltpu.VMEM(weight.shape, f32),
            pltpu.VMEM(weight.shape, f32),
            pltpu.SemaphoreType.DMA((4,)),
        ],
        compiler_params=params(8),
        cost_estimate=pl.CostEstimate(flops=0, bytes_accessed=0, transcendentals=0),
        name="leaving_blocks",
    )(dests, weight, one, two)


def line_gather(own, axis):
    n = lax.axis_size(axis)
    below, above = [own], [own]
    for step in range(1, n):
        below.append(lax.ppermute(below[-1], axis, [(i, i + 1) for i in range(step - 1, n - 1)]))
        above.append(lax.ppermute(above[-1], axis, [(i + 1, i) for i in range(n - step)]))
    return (*below[1:], *above[1:])


def backward_kernel(kept, ids, slices, *refs):
    count = len(ids)
    packs, up_ref = refs[:count], refs[count]
    acc, meta_ref, *far_ref = refs[count + 1 : -2]
    meta_s, sem = refs[-2:]
    side = packs[0].shape[1]
    pitch = side + TILE
    width = acc.shape[1] // slices
    for at, ident in enumerate(ids):
        for s in range(kept):
            tile = packs[at][s * pitch + side : (s + 1) * pitch, :].astype(f32)
            row = ident * kept + s
            meta_ref[row : row + 1, :] = tile[0:1, :].astype(jnp.int32)
    copy = pltpu.make_async_copy(meta_ref, meta_s, sem)
    copy.start()
    acc[...] = jnp.zeros_like(acc)
    copy.wait()
    for at, ident in enumerate(ids):
        for s in range(kept):
            row = meta_s[ident * kept + s, 0]
            col = meta_s[ident * kept + s, 1]
            part = lax.dot_general(
                lanes(up_ref, col, side),
                packs[at][s * pitch : s * pitch + side, :],
                (((1,), (1,)), ((), ())),
                preferred_element_type=f32,
            )
            place = pl.ds(pl.multiple_of(row * side, side), side)
            acc[:, place] = acc[:, place] + part
    for ref in far_ref:
        far = share_order(lax.axis_index("mp"), slices)[1]
        ref[...] = (lanes(acc, far, width) * grad_scale).astype(bf16)


def split_kernel(slices, chosen, acc, *shares):
    width = acc.shape[1] // slices
    order = share_order(lax.axis_index("mp"), slices)
    for ref, k in zip(shares, chosen):
        ref[...] = (lanes(acc, order[k], width) * grad_scale).astype(ref.dtype)


def split(acc, slices, chosen):
    shape = (acc.shape[0], acc.shape[1] // slices)
    return pl.pallas_call(
        functools.partial(split_kernel, slices, chosen),
        out_shape=tuple(jax.ShapeDtypeStruct(shape, bf16 if k else f32) for k in chosen),
        in_specs=[VMEM],
        out_specs=(VMEM,) * len(chosen),
        compiler_params=params(),
        cost_estimate=pl.CostEstimate(flops=0, bytes_accessed=0, transcendentals=0),
        name="split_shares",
    )(acc)


def share_order(me, slices):
    if slices == 4:
        low = me < 2
        return (me, jnp.where(low, 3, 0), jnp.where(low, 2, 1), jnp.bitwise_xor(me, 1))
    return tuple(lax.rem(me + k, slices) for k in range(slices))


def backward(packs, ids, upstream, kept, slices, features):
    tokens = upstream.shape[0]
    side = packs[0].shape[1]
    blocks = len(ids) * kept
    far = [jax.ShapeDtypeStruct((tokens, features), bf16)] * (slices == 4)
    return pl.pallas_call(
        functools.partial(backward_kernel, kept, ids, slices),
        out_shape=(
            jax.ShapeDtypeStruct((tokens, slices * features), f32),
            jax.ShapeDtypeStruct((blocks, side), jnp.int32),
            *far,
        ),
        in_specs=[VMEM] * (len(ids) + 1),
        out_specs=(VMEM,) * (2 + len(far)),
        scratch_shapes=[pltpu.SMEM((blocks, side), jnp.int32), pltpu.SemaphoreType.DMA],
        compiler_params=params(),
        cost_estimate=pl.CostEstimate(flops=0, bytes_accessed=0, transcendentals=0),
        name="input_gradient",
    )(*packs, upstream)


def line_reduce(shares, axis):
    n = len(shares)
    right = left = None
    for step in range(1, n):
        to_right, to_left = shares[n - step], shares[step]
        if right is not None:
            to_right = (to_right.astype(f32) + right.astype(f32)).astype(bf16)
            to_left = (to_left.astype(f32) + left.astype(f32)).astype(bf16)
        right = lax.ppermute(to_right, axis, [(i, i + 1) for i in range(step)])
        left = lax.ppermute(to_left, axis, [(n - 1 - i, n - 2 - i) for i in range(step)])
    if right is None:
        return shares[0].astype(bf16)
    return (shares[0] + right.astype(f32) + left.astype(f32)).astype(bf16)


def after(value, *others):
    return lax.optimization_barrier((value, *others))[0]


def sum_kernel(far_h, came_h, sum_ref, far_ref, came_ref, sems):
    @pl.when(lax.rem(lax.axis_index("mp"), 3) != 0)
    def _():
        copies = [
            pltpu.make_async_copy(far_h, far_ref, sems.at[0]),
            pltpu.make_async_copy(came_h, came_ref, sems.at[1]),
        ]
        for copy in copies:
            copy.start()
        for copy in copies:
            copy.wait()
        sum_ref[...] = (far_ref[...].astype(f32) + came_ref[...].astype(f32)).astype(bf16)


def inner_sum(far, came):
    return pl.pallas_call(
        sum_kernel,
        out_shape=jax.ShapeDtypeStruct(far.shape, bf16),
        in_specs=[ANY] * 2,
        out_specs=VMEM,
        scratch_shapes=[
            pltpu.VMEM(far.shape, bf16),
            pltpu.VMEM(far.shape, bf16),
            pltpu.SemaphoreType.DMA((2,)),
        ],
        compiler_params=params(),
        cost_estimate=pl.CostEstimate(flops=0, bytes_accessed=0, transcendentals=0),
        name="inner_sum",
    )(far, came)


def choose_kernel(outer_h, inner_h, mixed_ref, sem):
    outer = lax.rem(lax.axis_index("mp"), 3) == 0
    for when, source in ((outer, outer_h), (jnp.logical_not(outer), inner_h)):

        @pl.when(when)
        def _(source=source):
            copy = pltpu.make_async_copy(source, mixed_ref, sem)
            copy.start()
            copy.wait()


def choose(at_outer, at_inner):
    return pl.pallas_call(
        choose_kernel,
        out_shape=jax.ShapeDtypeStruct(at_outer.shape, bf16),
        in_specs=[ANY] * 2,
        out_specs=VMEM,
        scratch_shapes=[pltpu.SemaphoreType.DMA],
        compiler_params=params(),
        cost_estimate=pl.CostEstimate(flops=0, bytes_accessed=0, transcendentals=0),
        name="choose_sent",
    )(at_outer, at_inner)


def plus(share, came):
    return (share.astype(f32) + came.astype(f32)).astype(bf16)


def token_copies(slices, own, came, x_ref, sems):
    me = lax.axis_index("mp")
    todo = [(None, own, me)]
    if slices == 4:
        near, middle, near_on, mixed = came
        outer = lax.rem(me, 3) == 0
        todo.append((None, near, jnp.bitwise_xor(me, 1)))
        todo.append((outer, mixed, jnp.where(me == 0, 2, 1)))
        todo.append((jnp.logical_not(outer), middle, 3 - me))
        todo.append((jnp.logical_not(outer), near_on, jnp.where(me == 1, 3, 0)))
    else:
        for k in range(1, slices):
            todo.append((me >= k, came[k - 1], jnp.maximum(me - k, 0)))
            todo.append((me + k < slices, came[slices + k - 2], jnp.minimum(me + k, slices - 1)))
    return [
        (when, pltpu.make_async_copy(source, x_ref.at[at], sems.at[i]))
        for i, (when, source, at) in enumerate(todo)
    ]


def run(when, action):
    if when is None:
        action()
    else:
        pl.when(when)(action)


def assemble_kernel(slices, own_h, *refs):
    came, (x_ref, sems) = refs[:-2], refs[-2:]
    copies = token_copies(slices, own_h, came, x_ref, sems)
    for when, copy in copies:
        run(when, copy.start)
    for when, copy in copies:
        run(when, copy.wait)


def assemble(own, came, slices):
    return pl.pallas_call(
        functools.partial(assemble_kernel, slices),
        out_shape=jax.ShapeDtypeStruct((slices, *own.shape), bf16),
        in_specs=[ANY] * (1 + len(came)),
        out_specs=VMEM,
        scratch_shapes=[pltpu.SemaphoreType.DMA((len(came) + 1,))],
        compiler_params=params(),
        cost_estimate=pl.CostEstimate(flops=0, bytes_accessed=0, transcendentals=0),
        name="assemble_tokens",
    )(own, *came)


def token_block(x_ref, last, row, side):
    per = x_ref.shape[2] // side
    place = pl.ds(pl.multiple_of((row % per) * side, side), side)
    block = x_ref[row // per, :, place]
    if last:
        me = lax.axis_index("mp")
        far_end = (lax.rem(me, 3) == 0) & (row // per == 3 - me)
        block = jnp.where(far_end, last[0][:, place], block)
    return block


def turn_kernel(meta_s, up_ref, turned_ref):
    side = turned_ref.shape[1]
    for b in range(turned_ref.shape[0]):
        turned_ref[b] = jnp.transpose(lanes(up_ref, meta_s[b, 1], side))


def turn(meta, upstream):
    blocks, side = meta.shape
    return pl.pallas_call(
        turn_kernel,
        out_shape=jax.ShapeDtypeStruct((blocks, side, upstream.shape[0]), bf16),
        in_specs=[SMEM, VMEM],
        out_specs=VMEM,
        compiler_params=params(),
        cost_estimate=pl.CostEstimate(flops=0, bytes_accessed=0, transcendentals=0),
        name="turn_upstream",
    )(meta, upstream)


def gradient_kernel(kept, dp, meta_s, turned_ref, x_ref, *refs):
    last, (store, send_ref) = refs[:-2], refs[-2:]
    side = store.shape[2]
    blocks = dp * kept
    half = blocks // 2
    me = lax.axis_index("dp")
    for b in range(blocks):
        row, dest = meta_s[b, 0], meta_s[b, 2]
        grad = jnp.dot(
            turned_ref[b], token_block(x_ref, last, row, side), preferred_element_type=f32
        )
        gap = jnp.bitwise_xor(jnp.maximum(dest, 0) // kept, me)
        place = (gap & 1) * (dp // 2) + lax.shift_right_logical(gap, 1)
        slot = jnp.where(dest >= 0, place * kept + jnp.maximum(dest, 0) % kept, blocks)
        store[slot] = grad * grad_scale
    send_ref[...] = store[half : 2 * half].astype(bf16)


def gradient(meta, x_all, last, turned, kept, dp):
    side = meta.shape[1]
    blocks = dp * kept
    half = blocks // 2
    return pl.pallas_call(
        functools.partial(gradient_kernel, kept, dp),
        out_shape=(
            jax.ShapeDtypeStruct((blocks + 1, side, side), f32),
            jax.ShapeDtypeStruct((half, side, side), bf16),
        ),
        in_specs=[SMEM] + [VMEM] * (2 + len(last)),
        out_specs=(VMEM, VMEM),
        compiler_params=params(),
        cost_estimate=pl.CostEstimate(flops=0, bytes_accessed=0, transcendentals=0),
        name="weight_gradient",
    )(meta, turned, x_all, *last)


def slot_reduce(keep, send, kept, dp):
    came = lax.ppermute(send, "dp", [(i, i ^ 1) for i in range(dp)])
    total = keep[: send.shape[0]] + came.astype(f32)
    totals = [total[:kept]]
    for gap in range(1, dp // 2):
        totals.append(total[gap * kept : (gap + 1) * kept].astype(bf16))
    parts = totals[:1]
    for gap in range(1, dp // 2):
        parts.append(lax.ppermute(totals[gap], "dp", [(i, i ^ (2 * gap)) for i in range(dp)]))
    return parts, totals


def forward_kernel(kept, ids, meta_s, *refs):
    count = len(ids)
    packs, x_ref, last, (out_ref, acc) = refs[:count], refs[count], refs[count + 1 : -2], refs[-2:]
    side = packs[0].shape[1]
    pitch = side + TILE
    acc[...] = jnp.zeros_like(acc)
    for at, ident in enumerate(ids):
        for s in range(kept):
            row = meta_s[ident * kept + s, 0]
            col = meta_s[ident * kept + s, 1]
            part = jnp.dot(
                token_block(x_ref, last, row, side),
                packs[at][s * pitch : s * pitch + side, :],
                preferred_element_type=f32,
            )
            place = pl.ds(pl.multiple_of(col * side, side), side)
            acc[:, place] = acc[:, place] + part
    out_ref[...] = (acc[...] * grad_scale).astype(bf16)


def forward(meta, packs, ids, x_all, last, kept, hidden):
    tokens = x_all.shape[1]
    return pl.pallas_call(
        functools.partial(forward_kernel, kept, ids),
        out_shape=jax.ShapeDtypeStruct((tokens, hidden), bf16),
        in_specs=[SMEM] + [VMEM] * (len(ids) + 1 + len(last)),
        out_specs=VMEM,
        scratch_shapes=[pltpu.VMEM((tokens, hidden), f32)],
        compiler_params=params(),
        cost_estimate=pl.CostEstimate(flops=0, bytes_accessed=0, transcendentals=0),
        name="hidden_out",
    )(meta, *packs, x_all, *last)


def finish_kernel(own_ref, first_ref, second_ref, out_ref):
    total = own_ref[...] + first_ref[...].astype(f32) + second_ref[...].astype(f32)
    out_ref[...] = total.astype(bf16)


def finish(own, first, second):
    return pl.pallas_call(
        finish_kernel,
        out_shape=jax.ShapeDtypeStruct(own.shape, bf16),
        in_specs=[VMEM] * 3,
        out_specs=VMEM,
        compiler_params=params(),
        cost_estimate=pl.CostEstimate(flops=0, bytes_accessed=0, transcendentals=0),
        name="finish_input_grad",
    )(own, first, second)


def update_kernel(
    dp, meta_s, w_ref, one_ref, two_ref, left_ref, right_ref, *refs
):
    parts, (new_w, new_one, new_two) = refs[:-3], refs[-3:]
    kept, side = w_ref.shape[0], w_ref.shape[1]
    travel = 3 * side
    me = lax.axis_index("dp")
    source = [jnp.int32(-1)] * kept

    def place(source, dest, here, code):
        mine = here & (dest >= 0) & (jnp.maximum(dest, 0) // kept == me)
        slot = jnp.maximum(dest, 0) % kept
        found = [jnp.where(mine & (slot == q), code, source[q]) for q in range(kept)]
        return found, code + mine.astype(jnp.int32)

    for s in range(kept):
        source, _ = place(source, meta_s[s, 2], True, jnp.int32(s))
    for side_at, other in ((kept, me - 1), (kept + kept // 2, me + 1)):
        here = (other >= 0) & (other < dp)
        gap = jnp.where(here, jnp.bitwise_xor(jnp.clip(other, 0, dp - 1), me), 0)
        code = jnp.int32(side_at)
        for s in range(kept):
            source, code = place(source, meta_s[gap * kept + s, 2], here, code)

    for q in range(kept):

        def write(weight, one, two, q=q):
            grad = parts[0][q]
            for part in parts[1:]:
                grad = grad + part[q].astype(f32)
            grad = jnp.transpose(grad)
            first = beta_first * one + (1.0 - beta_first) * grad
            second = beta_second * two + (1.0 - beta_second) * grad * grad
            stepped = weight - learn_rate * first / (jnp.sqrt(second) + epsilon)
            new_w[q] = stepped.astype(bf16)
            new_one[q] = first
            new_two[q] = second

        @pl.when(source[q] < 0)
        def _(q=q):
            new_w[q] = jnp.zeros((side, side), bf16)
            new_one[q] = jnp.zeros((side, side), f32)
            new_two[q] = jnp.zeros((side, side), f32)

        @pl.when((source[q] >= 0) & (source[q] < kept))
        def _(q=q):
            s = jnp.clip(source[q], 0, kept - 1)
            write(w_ref[s].astype(f32), one_ref[s], two_ref[s])

        for ref, first_code in ((left_ref, kept), (right_ref, kept + kept // 2)):

            @pl.when((source[q] >= first_code) & (source[q] < first_code + kept // 2))
            def _(q=q, ref=ref, first_code=first_code):
                rank = jnp.clip(source[q] - first_code, 0, kept // 2 - 1)
                base = pl.multiple_of(rank * travel, TILE)
                write(
                    ref[pl.ds(base, side), :].astype(f32),
                    ref[pl.ds(base + side, side), :].astype(f32),
                    ref[pl.ds(base + 2 * side, side), :].astype(f32),
                )


def update(meta, parts, weight, one, two, from_left, from_right, dp):
    shape = weight.shape
    return pl.pallas_call(
        functools.partial(update_kernel, dp),
        out_shape=(
            jax.ShapeDtypeStruct(shape, bf16),
            jax.ShapeDtypeStruct(shape, f32),
            jax.ShapeDtypeStruct(shape, f32),
        ),
        in_specs=[SMEM] + [VMEM] * (5 + len(parts)),
        out_specs=(VMEM,) * 3,
        compiler_params=params(),
        cost_estimate=pl.CostEstimate(flops=0, bytes_accessed=0, transcendentals=0),
        name="adam_update",
    )(meta, weight, one, two, from_left, from_right, *parts)


def body(weight, moment_one, moment_two, block_row, block_col, dest_slot, tokens, upstream):
    kept = weight.shape[0]
    dp = lax.axis_size("dp")
    slices = lax.axis_size("mp")
    four = slices == 4
    pairs, inner = [(0, 1), (1, 0), (2, 3), (3, 2)], [(1, 2), (2, 1)]
    inward, outward = [(0, 1), (3, 2)], [(1, 0), (2, 3)]

    packs, ids = [pack(block_row, block_col, dest_slot, weight)], [0]
    if four:
        near = lax.ppermute(tokens, "mp", pairs)
        middle = lax.ppermute(tokens, "mp", inner)
    else:
        came = line_gather(tokens, "mp")
    for gap in range(2, dp, 2):
        packs.append(lax.ppermute(packs[0], "dp", [(i, i ^ gap) for i in range(dp)]))
        ids.append(gap)
    held = hold(after(upstream, packs[0]), packs[0])
    packs[0], up_held = held[1], held[0]
    packs[1:] = lax.optimization_barrier((*packs[1:], *held))[: len(packs) - 1]
    packs += [lax.ppermute(p, "dp", [(i, i ^ 1) for i in range(dp)]) for p in packs]
    ids = tuple(ids + [i ^ 1 for i in ids])
    sums, meta, *far = backward(packs, ids, up_held, kept, slices, tokens.shape[1])

    dest_leave = dest_slot
    if four:
        outer = lax.rem(lax.axis_index("mp"), 3) == 0
        near, middle, far = lax.optimization_barrier((near, middle, far[0]))
        mixed_sent = choose(far, middle)
        near, mixed = lax.optimization_barrier((near, mixed_sent))
        mixed = lax.ppermute(mixed, "mp", inward + outward)
        near_on = lax.ppermute(near, "mp", inner)
        own_share, second, first = split(after(sums, mixed_sent), slices, (0, 2, 3))
        sum_base = after(far, own_share)
    if four:
        sum_far = inner_sum(sum_base, mixed)
        mixed_on = choose(after(second, sum_far), near_on)
        sum_far, mixed_on = lax.optimization_barrier((sum_far, mixed_on))
        mixed_on = lax.ppermute(mixed_on, "mp", inward + outward)
        passed_far = lax.ppermute(sum_far, "mp", inner)
        came = (near, middle, near_on, mixed)
        x_all = assemble(after(tokens, sum_far), came, slices)
        turned = turn(after(meta, x_all), upstream)
        dest_leave = after(dest_slot, turned)
        last = (mixed_on,)
    else:
        x_all, last = assemble(tokens, came, slices), ()
        turned = turn(meta, upstream)
    to_left, to_right = leave(dest_leave, weight, moment_one, moment_two)
    from_left = lax.ppermute(to_right, "dp", [(i, i + 1) for i in range(dp - 1)])
    from_right = lax.ppermute(to_left, "dp", [(i + 1, i) for i in range(dp - 1)])
    keep, send = gradient(meta, x_all, last, turned, kept, dp)
    parts, totals = slot_reduce(keep, send, kept, dp)
    meta_out = meta
    if four:
        sum_second = plus(after(second, send), mixed_on)
        sum_first = plus(after(first, send), passed_far)
        sum_second, sum_first = lax.optimization_barrier((sum_second, sum_first))
        passed_second = lax.ppermute(sum_second, "mp", inner)
        came_first = lax.ppermute(sum_first, "mp", inward + outward)
        meta_out = after(meta, sum_second, sum_first, *totals)
    hidden_out = forward(meta_out, packs, ids, x_all, last, kept, upstream.shape[1])
    new_weight, new_first, new_second = update(
        meta, parts, weight, moment_one, moment_two, from_left, from_right, dp
    )
    if four:
        input_grad = finish(
            after(own_share, hidden_out, new_weight), came_first, passed_second
        )
    else:
        input_grad = line_reduce(split(sums, slices, tuple(range(slices))), "mp")
    return (new_weight, new_first, new_second, hidden_out, input_grad)


def solution(mesh):
    blocks = P(("dp", "mp"), None, None)
    ints = P(("dp", "mp"))
    acts = P("dp", "mp")
    return jax.shard_map(
        body,
        mesh=mesh,
        in_specs=(blocks, blocks, blocks, ints, ints, ints, acts, acts),
        out_specs=(blocks, blocks, blocks, acts, acts),
        check_vma=False,
    )
```

```python
import functools
import math

import jax
import jax.numpy as jnp
from jax import lax
from jax.experimental import pallas as pl
from jax.experimental.pallas import tpu as pltpu
from jax.sharding import PartitionSpec as P

D = 8192
TILE = 16

learn_rate = 0.02
beta_first = 0.9
beta_second = 0.95
epsilon = 1e-08
grad_scale = 1.0 / math.sqrt(D)

f32 = jnp.float32
bf16 = jnp.bfloat16
VMEM = pl.BlockSpec(memory_space=pltpu.VMEM)
ANY = pl.BlockSpec(memory_space=pl.ANY)
SMEM = pl.BlockSpec(memory_space=pltpu.SMEM)


def params(mib=24):
    return pltpu.CompilerParams(vmem_limit_bytes=mib * 1024 * 1024)


def lanes(ref, index, width):
    return ref[:, pl.ds(pl.multiple_of(index * width, width), width)]


def pack_kernel(row_h, col_h, dest_h, w_h, pack_ref, row_s, col_s, dest_s, sems):
    kept, side = w_h.shape[0], w_h.shape[1]
    pitch = side + TILE
    names = [
        pltpu.make_async_copy(source, target, sems.at[i])
        for i, (source, target) in enumerate(((row_h, row_s), (col_h, col_s), (dest_h, dest_s)))
    ]
    blocks = [
        pltpu.make_async_copy(w_h.at[s], pack_ref.at[pl.ds(s * pitch, side)], sems.at[3 + s])
        for s in range(kept)
    ]
    for copy in names + blocks:
        copy.start()
    for copy in names:
        copy.wait()
    lane = lax.broadcasted_iota(jnp.int32, (TILE, side), 1)
    for s in range(kept):
        tile = jnp.where(lane == 0, row_s[s], jnp.where(lane == 1, col_s[s], dest_s[s]))
        pack_ref[s * pitch + side : (s + 1) * pitch, :] = tile.astype(f32).astype(bf16)
    for copy in blocks:
        copy.wait()


def pack(rows, cols, dests, weight):
    kept, side, _ = weight.shape
    return pl.pallas_call(
        pack_kernel,
        out_shape=jax.ShapeDtypeStruct((kept * (side + TILE), side), bf16),
        in_specs=[ANY] * 4,
        out_specs=VMEM,
        scratch_shapes=[pltpu.SMEM((kept,), jnp.int32)] * 3
        + [pltpu.SemaphoreType.DMA((3 + kept,))],
        compiler_params=params(60),
        cost_estimate=pl.CostEstimate(flops=0, bytes_accessed=0, transcendentals=0),
        name="pack_blocks",
    )(rows, cols, dests, weight)


def hold_kernel(count, *refs):
    sems = refs[-1]
    copies = [
        pltpu.make_async_copy(refs[i], refs[count + i], sems.at[i]) for i in range(count)
    ]
    for copy in copies:
        copy.start()
    for copy in copies:
        copy.wait()


def hold(*arrays):
    count = len(arrays)
    return pl.pallas_call(
        functools.partial(hold_kernel, count),
        out_shape=tuple(jax.ShapeDtypeStruct(a.shape, a.dtype) for a in arrays),
        in_specs=[ANY] * count,
        out_specs=(VMEM,) * count,
        scratch_shapes=[pltpu.SemaphoreType.DMA((count,))],
        compiler_params=params(8),
        cost_estimate=pl.CostEstimate(flops=0, bytes_accessed=0, transcendentals=0),
        name="hold_arrays",
    )(*arrays)


def leave_kernel(dest_h, w_h, one_h, two_h, left_ref, right_ref, dest_s, w_ref, one_ref, two_ref, sems):
    kept, side = w_ref.shape[0], w_ref.shape[1]
    half = kept // 2
    me = lax.axis_index("dp")
    travel = 3 * side
    copies = [
        pltpu.make_async_copy(source, target, sems.at[i])
        for i, (source, target) in enumerate(
            ((dest_h, dest_s), (w_h, w_ref), (one_h, one_ref), (two_h, two_ref))
        )
    ]
    for copy in copies:
        copy.start()
    left_ref[...] = jnp.zeros_like(left_ref)
    right_ref[...] = jnp.zeros_like(right_ref)
    for copy in copies:
        copy.wait()
    to_left = jnp.int32(0)
    to_right = jnp.int32(0)
    for s in range(kept):
        dest = dest_s[s]
        goal = jnp.where(dest >= 0, dest // kept, me)
        for ref, count, going in (
            (left_ref, to_left, goal < me),
            (right_ref, to_right, goal > me),
        ):

            @pl.when(going)
            def _(ref=ref, count=count, s=s):
                base = pl.multiple_of(jnp.minimum(count, half - 1) * travel, TILE)
                ref[pl.ds(base, side), :] = w_ref[s]
                ref[pl.ds(base + side, side), :] = one_ref[s].astype(bf16)
                ref[pl.ds(base + 2 * side, side), :] = two_ref[s].astype(bf16)

        to_left = to_left + (goal < me).astype(jnp.int32)
        to_right = to_right + (goal > me).astype(jnp.int32)


def leave(dests, weight, one, two):
    kept, side, _ = weight.shape
    travel = jax.ShapeDtypeStruct((kept // 2 * 3 * side, side), bf16)
    return pl.pallas_call(
        leave_kernel,
        out_shape=(travel, travel),
        in_specs=[ANY] * 4,
        out_specs=(VMEM, VMEM),
        scratch_shapes=[
            pltpu.SMEM((kept,), jnp.int32),
            pltpu.VMEM(weight.shape, bf16),
            pltpu.VMEM(weight.shape, f32),
            pltpu.VMEM(weight.shape, f32),
            pltpu.SemaphoreType.DMA((4,)),
        ],
        compiler_params=params(8),
        cost_estimate=pl.CostEstimate(flops=0, bytes_accessed=0, transcendentals=0),
        name="leaving_blocks",
    )(dests, weight, one, two)


def line_gather(own, axis):
    n = lax.axis_size(axis)
    below, above = [own], [own]
    for step in range(1, n):
        below.append(lax.ppermute(below[-1], axis, [(i, i + 1) for i in range(step - 1, n - 1)]))
        above.append(lax.ppermute(above[-1], axis, [(i + 1, i) for i in range(n - step)]))
    return (*below[1:], *above[1:])


def backward_kernel(kept, ids, slices, *refs):
    count = len(ids)
    packs, up_ref = refs[:count], refs[count]
    acc, meta_ref, *far_ref = refs[count + 1 : -2]
    meta_s, sem = refs[-2:]
    side = packs[0].shape[1]
    pitch = side + TILE
    width = acc.shape[1] // slices
    for at, ident in enumerate(ids):
        for s in range(kept):
            tile = packs[at][s * pitch + side : (s + 1) * pitch, :].astype(f32)
            row = ident * kept + s
            meta_ref[row : row + 1, :] = tile[0:1, :].astype(jnp.int32)
    copy = pltpu.make_async_copy(meta_ref, meta_s, sem)
    copy.start()
    acc[...] = jnp.zeros_like(acc)
    copy.wait()
    for at, ident in enumerate(ids):
        for s in range(kept):
            row = meta_s[ident * kept + s, 0]
            col = meta_s[ident * kept + s, 1]
            part = lax.dot_general(
                lanes(up_ref, col, side),
                packs[at][s * pitch : s * pitch + side, :],
                (((1,), (1,)), ((), ())),
                preferred_element_type=f32,
            )
            place = pl.ds(pl.multiple_of(row * side, side), side)
            acc[:, place] = acc[:, place] + part
    for ref in far_ref:
        far = share_order(lax.axis_index("mp"), slices)[1]
        ref[...] = (lanes(acc, far, width) * grad_scale).astype(bf16)


def split_kernel(slices, chosen, acc, *shares):
    width = acc.shape[1] // slices
    order = share_order(lax.axis_index("mp"), slices)
    for ref, k in zip(shares, chosen):
        ref[...] = (lanes(acc, order[k], width) * grad_scale).astype(ref.dtype)


def split(acc, slices, chosen):
    shape = (acc.shape[0], acc.shape[1] // slices)
    return pl.pallas_call(
        functools.partial(split_kernel, slices, chosen),
        out_shape=tuple(jax.ShapeDtypeStruct(shape, bf16 if k else f32) for k in chosen),
        in_specs=[VMEM],
        out_specs=(VMEM,) * len(chosen),
        compiler_params=params(),
        cost_estimate=pl.CostEstimate(flops=0, bytes_accessed=0, transcendentals=0),
        name="split_shares",
    )(acc)


def share_order(me, slices):
    if slices == 4:
        low = me < 2
        return (me, jnp.where(low, 3, 0), jnp.where(low, 2, 1), jnp.bitwise_xor(me, 1))
    return tuple(lax.rem(me + k, slices) for k in range(slices))


def backward(packs, ids, upstream, kept, slices, features):
    tokens = upstream.shape[0]
    side = packs[0].shape[1]
    blocks = len(ids) * kept
    far = [jax.ShapeDtypeStruct((tokens, features), bf16)] * (slices == 4)
    return pl.pallas_call(
        functools.partial(backward_kernel, kept, ids, slices),
        out_shape=(
            jax.ShapeDtypeStruct((tokens, slices * features), f32),
            jax.ShapeDtypeStruct((blocks, side), jnp.int32),
            *far,
        ),
        in_specs=[VMEM] * (len(ids) + 1),
        out_specs=(VMEM,) * (2 + len(far)),
        scratch_shapes=[pltpu.SMEM((blocks, side), jnp.int32), pltpu.SemaphoreType.DMA],
        compiler_params=params(),
        cost_estimate=pl.CostEstimate(flops=0, bytes_accessed=0, transcendentals=0),
        name="input_gradient",
    )(*packs, upstream)


def line_reduce(shares, axis):
    n = len(shares)
    right = left = None
    for step in range(1, n):
        to_right, to_left = shares[n - step], shares[step]
        if right is not None:
            to_right = (to_right.astype(f32) + right.astype(f32)).astype(bf16)
            to_left = (to_left.astype(f32) + left.astype(f32)).astype(bf16)
        right = lax.ppermute(to_right, axis, [(i, i + 1) for i in range(step)])
        left = lax.ppermute(to_left, axis, [(n - 1 - i, n - 2 - i) for i in range(step)])
    if right is None:
        return shares[0].astype(bf16)
    return (shares[0] + right.astype(f32) + left.astype(f32)).astype(bf16)


def after(value, *others):
    return lax.optimization_barrier((value, *others))[0]


def sum_kernel(far_h, came_h, sum_ref, far_ref, came_ref, sems):
    @pl.when(lax.rem(lax.axis_index("mp"), 3) != 0)
    def _():
        copies = [
            pltpu.make_async_copy(far_h, far_ref, sems.at[0]),
            pltpu.make_async_copy(came_h, came_ref, sems.at[1]),
        ]
        for copy in copies:
            copy.start()
        for copy in copies:
            copy.wait()
        sum_ref[...] = (far_ref[...].astype(f32) + came_ref[...].astype(f32)).astype(bf16)


def inner_sum(far, came):
    return pl.pallas_call(
        sum_kernel,
        out_shape=jax.ShapeDtypeStruct(far.shape, bf16),
        in_specs=[ANY] * 2,
        out_specs=VMEM,
        scratch_shapes=[
            pltpu.VMEM(far.shape, bf16),
            pltpu.VMEM(far.shape, bf16),
            pltpu.SemaphoreType.DMA((2,)),
        ],
        compiler_params=params(),
        cost_estimate=pl.CostEstimate(flops=0, bytes_accessed=0, transcendentals=0),
        name="inner_sum",
    )(far, came)


def choose_kernel(outer_h, inner_h, mixed_ref, sem):
    outer = lax.rem(lax.axis_index("mp"), 3) == 0
    for when, source in ((outer, outer_h), (jnp.logical_not(outer), inner_h)):

        @pl.when(when)
        def _(source=source):
            copy = pltpu.make_async_copy(source, mixed_ref, sem)
            copy.start()
            copy.wait()


def choose(at_outer, at_inner):
    return pl.pallas_call(
        choose_kernel,
        out_shape=jax.ShapeDtypeStruct(at_outer.shape, bf16),
        in_specs=[ANY] * 2,
        out_specs=VMEM,
        scratch_shapes=[pltpu.SemaphoreType.DMA],
        compiler_params=params(),
        cost_estimate=pl.CostEstimate(flops=0, bytes_accessed=0, transcendentals=0),
        name="choose_sent",
    )(at_outer, at_inner)


def plus(share, came):
    return (share.astype(f32) + came.astype(f32)).astype(bf16)


def token_copies(slices, own, came, x_ref, sems):
    me = lax.axis_index("mp")
    todo = [(None, own, me)]
    if slices == 4:
        near, middle, near_on, mixed = came
        outer = lax.rem(me, 3) == 0
        todo.append((None, near, jnp.bitwise_xor(me, 1)))
        todo.append((outer, mixed, jnp.where(me == 0, 2, 1)))
        todo.append((jnp.logical_not(outer), middle, 3 - me))
        todo.append((jnp.logical_not(outer), near_on, jnp.where(me == 1, 3, 0)))
    else:
        for k in range(1, slices):
            todo.append((me >= k, came[k - 1], jnp.maximum(me - k, 0)))
            todo.append((me + k < slices, came[slices + k - 2], jnp.minimum(me + k, slices - 1)))
    return [
        (when, pltpu.make_async_copy(source, x_ref.at[at], sems.at[i]))
        for i, (when, source, at) in enumerate(todo)
    ]


def run(when, action):
    if when is None:
        action()
    else:
        pl.when(when)(action)


def assemble_kernel(slices, own_h, *refs):
    came, (x_ref, sems) = refs[:-2], refs[-2:]
    copies = token_copies(slices, own_h, came, x_ref, sems)
    for when, copy in copies:
        run(when, copy.start)
    for when, copy in copies:
        run(when, copy.wait)


def assemble(own, came, slices):
    return pl.pallas_call(
        functools.partial(assemble_kernel, slices),
        out_shape=jax.ShapeDtypeStruct((slices, *own.shape), bf16),
        in_specs=[ANY] * (1 + len(came)),
        out_specs=VMEM,
        scratch_shapes=[pltpu.SemaphoreType.DMA((len(came) + 1,))],
        compiler_params=params(),
        cost_estimate=pl.CostEstimate(flops=0, bytes_accessed=0, transcendentals=0),
        name="assemble_tokens",
    )(own, *came)


def token_block(x_ref, last, row, side):
    per = x_ref.shape[2] // side
    place = pl.ds(pl.multiple_of((row % per) * side, side), side)
    block = x_ref[row // per, :, place]
    if last:
        me = lax.axis_index("mp")
        far_end = (lax.rem(me, 3) == 0) & (row // per == 3 - me)
        block = jnp.where(far_end, last[0][:, place], block)
    return block


def turn_kernel(meta_s, up_ref, turned_ref):
    side = turned_ref.shape[1]
    for b in range(turned_ref.shape[0]):
        turned_ref[b] = jnp.transpose(lanes(up_ref, meta_s[b, 1], side))


def turn(meta, upstream):
    blocks, side = meta.shape
    return pl.pallas_call(
        turn_kernel,
        out_shape=jax.ShapeDtypeStruct((blocks, side, upstream.shape[0]), bf16),
        in_specs=[SMEM, VMEM],
        out_specs=VMEM,
        compiler_params=params(),
        cost_estimate=pl.CostEstimate(flops=0, bytes_accessed=0, transcendentals=0),
        name="turn_upstream",
    )(meta, upstream)


def gradient_kernel(kept, dp, meta_s, turned_ref, x_ref, *refs):
    last, (store, send_ref) = refs[:-2], refs[-2:]
    side = store.shape[2]
    blocks = dp * kept
    half = blocks // 2
    me = lax.axis_index("dp")
    for b in range(blocks):
        row, dest = meta_s[b, 0], meta_s[b, 2]
        grad = jnp.dot(
            turned_ref[b], token_block(x_ref, last, row, side), preferred_element_type=f32
        )
        gap = jnp.bitwise_xor(jnp.maximum(dest, 0) // kept, me)
        place = (gap & 1) * (dp // 2) + lax.shift_right_logical(gap, 1)
        slot = jnp.where(dest >= 0, place * kept + jnp.maximum(dest, 0) % kept, blocks)
        store[slot] = grad * grad_scale
    send_ref[...] = store[half : 2 * half].astype(bf16)


def gradient(meta, x_all, last, turned, kept, dp):
    side = meta.shape[1]
    blocks = dp * kept
    half = blocks // 2
    return pl.pallas_call(
        functools.partial(gradient_kernel, kept, dp),
        out_shape=(
            jax.ShapeDtypeStruct((blocks + 1, side, side), f32),
            jax.ShapeDtypeStruct((half, side, side), bf16),
        ),
        in_specs=[SMEM] + [VMEM] * (2 + len(last)),
        out_specs=(VMEM, VMEM),
        compiler_params=params(),
        cost_estimate=pl.CostEstimate(flops=0, bytes_accessed=0, transcendentals=0),
        name="weight_gradient",
    )(meta, turned, x_all, *last)


def slot_reduce(keep, send, kept, dp):
    came = lax.ppermute(send, "dp", [(i, i ^ 1) for i in range(dp)])
    total = keep[: send.shape[0]] + came.astype(f32)
    totals = [total[:kept]]
    for gap in range(1, dp // 2):
        totals.append(total[gap * kept : (gap + 1) * kept].astype(bf16))
    parts = totals[:1]
    for gap in range(1, dp // 2):
        parts.append(lax.ppermute(totals[gap], "dp", [(i, i ^ (2 * gap)) for i in range(dp)]))
    return parts, totals


def forward_kernel(kept, ids, meta_s, *refs):
    count = len(ids)
    packs, x_ref, last, (out_ref, acc) = refs[:count], refs[count], refs[count + 1 : -2], refs[-2:]
    side = packs[0].shape[1]
    pitch = side + TILE
    acc[...] = jnp.zeros_like(acc)
    for at, ident in enumerate(ids):
        for s in range(kept):
            row = meta_s[ident * kept + s, 0]
            col = meta_s[ident * kept + s, 1]
            part = jnp.dot(
                token_block(x_ref, last, row, side),
                packs[at][s * pitch : s * pitch + side, :],
                preferred_element_type=f32,
            )
            place = pl.ds(pl.multiple_of(col * side, side), side)
            acc[:, place] = acc[:, place] + part
    out_ref[...] = (acc[...] * grad_scale).astype(bf16)


def forward(meta, packs, ids, x_all, last, kept, hidden):
    tokens = x_all.shape[1]
    return pl.pallas_call(
        functools.partial(forward_kernel, kept, ids),
        out_shape=jax.ShapeDtypeStruct((tokens, hidden), bf16),
        in_specs=[SMEM] + [VMEM] * (len(ids) + 1 + len(last)),
        out_specs=VMEM,
        scratch_shapes=[pltpu.VMEM((tokens, hidden), f32)],
        compiler_params=params(),
        cost_estimate=pl.CostEstimate(flops=0, bytes_accessed=0, transcendentals=0),
        name="hidden_out",
    )(meta, *packs, x_all, *last)


def finish_kernel(own_ref, first_ref, second_ref, out_ref):
    total = own_ref[...] + first_ref[...].astype(f32) + second_ref[...].astype(f32)
    out_ref[...] = total.astype(bf16)


def finish(own, first, second):
    return pl.pallas_call(
        finish_kernel,
        out_shape=jax.ShapeDtypeStruct(own.shape, bf16),
        in_specs=[VMEM] * 3,
        out_specs=VMEM,
        compiler_params=params(),
        cost_estimate=pl.CostEstimate(flops=0, bytes_accessed=0, transcendentals=0),
        name="finish_input_grad",
    )(own, first, second)


def update_kernel(
    dp, meta_s, w_ref, one_ref, two_ref, left_ref, right_ref, *refs
):
    parts, (new_w, new_one, new_two) = refs[:-3], refs[-3:]
    kept, side = w_ref.shape[0], w_ref.shape[1]
    travel = 3 * side
    me = lax.axis_index("dp")
    source = [jnp.int32(-1)] * kept

    def place(source, dest, here, code):
        mine = here & (dest >= 0) & (jnp.maximum(dest, 0) // kept == me)
        slot = jnp.maximum(dest, 0) % kept
        found = [jnp.where(mine & (slot == q), code, source[q]) for q in range(kept)]
        return found, code + mine.astype(jnp.int32)

    for s in range(kept):
        source, _ = place(source, meta_s[s, 2], True, jnp.int32(s))
    for side_at, other in ((kept, me - 1), (kept + kept // 2, me + 1)):
        here = (other >= 0) & (other < dp)
        gap = jnp.where(here, jnp.bitwise_xor(jnp.clip(other, 0, dp - 1), me), 0)
        code = jnp.int32(side_at)
        for s in range(kept):
            source, code = place(source, meta_s[gap * kept + s, 2], here, code)

    for q in range(kept):

        def write(weight, one, two, q=q):
            grad = parts[0][q]
            for part in parts[1:]:
                grad = grad + part[q].astype(f32)
            grad = jnp.transpose(grad)
            first = beta_first * one + (1.0 - beta_first) * grad
            second = beta_second * two + (1.0 - beta_second) * grad * grad
            stepped = weight - learn_rate * first / (jnp.sqrt(second) + epsilon)
            new_w[q] = stepped.astype(bf16)
            new_one[q] = first
            new_two[q] = second

        @pl.when(source[q] < 0)
        def _(q=q):
            new_w[q] = jnp.zeros((side, side), bf16)
            new_one[q] = jnp.zeros((side, side), f32)
            new_two[q] = jnp.zeros((side, side), f32)

        @pl.when((source[q] >= 0) & (source[q] < kept))
        def _(q=q):
            s = jnp.clip(source[q], 0, kept - 1)
            write(w_ref[s].astype(f32), one_ref[s], two_ref[s])

        for ref, first_code in ((left_ref, kept), (right_ref, kept + kept // 2)):

            @pl.when((source[q] >= first_code) & (source[q] < first_code + kept // 2))
            def _(q=q, ref=ref, first_code=first_code):
                rank = jnp.clip(source[q] - first_code, 0, kept // 2 - 1)
                base = pl.multiple_of(rank * travel, TILE)
                write(
                    ref[pl.ds(base, side), :].astype(f32),
                    ref[pl.ds(base + side, side), :].astype(f32),
                    ref[pl.ds(base + 2 * side, side), :].astype(f32),
                )


def update(meta, parts, weight, one, two, from_left, from_right, dp):
    shape = weight.shape
    return pl.pallas_call(
        functools.partial(update_kernel, dp),
        out_shape=(
            jax.ShapeDtypeStruct(shape, bf16),
            jax.ShapeDtypeStruct(shape, f32),
            jax.ShapeDtypeStruct(shape, f32),
        ),
        in_specs=[SMEM] + [VMEM] * (5 + len(parts)),
        out_specs=(VMEM,) * 3,
        compiler_params=params(),
        cost_estimate=pl.CostEstimate(flops=0, bytes_accessed=0, transcendentals=0),
        name="adam_update",
    )(meta, weight, one, two, from_left, from_right, *parts)


def body(weight, moment_one, moment_two, block_row, block_col, dest_slot, tokens, upstream):
    kept = weight.shape[0]
    dp = lax.axis_size("dp")
    slices = lax.axis_size("mp")
    four = slices == 4
    pairs, inner = [(0, 1), (1, 0), (2, 3), (3, 2)], [(1, 2), (2, 1)]
    inward, outward = [(0, 1), (3, 2)], [(1, 0), (2, 3)]

    packs, ids = [pack(block_row, block_col, dest_slot, weight)], [0]
    if four:
        near = lax.ppermute(tokens, "mp", pairs)
        middle = lax.ppermute(tokens, "mp", inner)
    else:
        came = line_gather(tokens, "mp")
    for gap in range(2, dp, 2):
        packs.append(lax.ppermute(packs[0], "dp", [(i, i ^ gap) for i in range(dp)]))
        ids.append(gap)
    held = hold(after(upstream, packs[0]), packs[0])
    packs[0], up_held = held[1], held[0]
    packs[1:] = lax.optimization_barrier((*packs[1:], *held))[: len(packs) - 1]
    packs += [lax.ppermute(p, "dp", [(i, i ^ 1) for i in range(dp)]) for p in packs]
    ids = tuple(ids + [i ^ 1 for i in ids])
    sums, meta, *far = backward(packs, ids, up_held, kept, slices, tokens.shape[1])

    dest_leave = dest_slot
    if four:
        outer = lax.rem(lax.axis_index("mp"), 3) == 0
        near, middle, far = lax.optimization_barrier((near, middle, far[0]))
        mixed_sent = choose(far, middle)
        near, mixed = lax.optimization_barrier((near, mixed_sent))
        mixed = lax.ppermute(mixed, "mp", inward + outward)
        near_on = lax.ppermute(near, "mp", inner)
        own_share, second, first = split(after(sums, mixed_sent), slices, (0, 2, 3))
        sum_base = after(far, own_share)
    if four:
        sum_far = inner_sum(sum_base, mixed)
        mixed_on = choose(after(second, sum_far), near_on)
        sum_far, mixed_on = lax.optimization_barrier((sum_far, mixed_on))
        mixed_on = lax.ppermute(mixed_on, "mp", inward + outward)
        passed_far = lax.ppermute(sum_far, "mp", inner)
        came = (near, middle, near_on, mixed)
        x_all = assemble(after(tokens, sum_far), came, slices)
        turned = turn(after(meta, x_all), upstream)
        dest_leave = after(dest_slot, turned)
        last = (mixed_on,)
    else:
        x_all, last = assemble(tokens, came, slices), ()
        turned = turn(meta, upstream)
    to_left, to_right = leave(dest_leave, weight, moment_one, moment_two)
    from_left = lax.ppermute(to_right, "dp", [(i, i + 1) for i in range(dp - 1)])
    from_right = lax.ppermute(to_left, "dp", [(i + 1, i) for i in range(dp - 1)])
    keep, send = gradient(meta, x_all, last, turned, kept, dp)
    parts, totals = slot_reduce(keep, send, kept, dp)
    meta_out = meta
    if four:
        sum_second = plus(after(second, send), mixed_on)
        sum_first = plus(after(first, send), passed_far)
        sum_second, sum_first = lax.optimization_barrier((sum_second, sum_first))
        passed_second = lax.ppermute(sum_second, "mp", inner)
        came_first = lax.ppermute(sum_first, "mp", inward + outward)
        meta_out = after(meta, sum_second, sum_first, *totals)
    hidden_out = forward(meta_out, packs, ids, x_all, last, kept, upstream.shape[1])
    new_weight, new_first, new_second = update(
        meta, parts, weight, moment_one, moment_two, from_left, from_right, dp
    )
    if four:
        input_grad = finish(
            after(own_share, hidden_out, new_weight), came_first, passed_second
        )
    else:
        input_grad = line_reduce(split(sums, slices, tuple(range(slices))), "mp")
    return (new_weight, new_first, new_second, hidden_out, input_grad)


def solution(mesh):
    blocks = P(("dp", "mp"), None, None)
    ints = P(("dp", "mp"))
    acts = P("dp", "mp")
    return jax.shard_map(
        body,
        mesh=mesh,
        in_specs=(blocks, blocks, blocks, ints, ints, ints, acts, acts),
        out_specs=(blocks, blocks, blocks, acts, acts),
        check_vma=False,
    )
```
